512 devices in a mesh: samp: 32 (over z, x_hi, core), par: 16 (over x_lo, y).
Axes of the slice: x: 4 (x_hi: 2, x_lo: 2; x = x_hi * 2 + x_lo), y: 8, z: 8, core: 2. Of those that a mesh axis runs over, the one named last changes fastest.
Arguments:
- activations: bfloat16 [512, 2, 64, 256], P('samp'), may hold values from 0 to 2
- cotangents: bfloat16 [512, 2, 64, 256], P('samp', None, 'par'), may hold values from -0.029907227 to 0.099609375
- energies: float32 [512], P('samp'), may hold values from -3 to -1
Outputs:
- update: float32 [64, 1152], P('par')
- coeffs: float32 [512], P('samp')
The draws below stay inside these ranges and needn't reach their ends.
All inputs are finite; a program needn't handle non-finite values.
Results may differ from the reference program's by a relative error of at most 0.0034.
Values may be sent and summed in bfloat16 or wider, within the bound.
A program may use at most 64 MiB of HBM per device.

```python
import math
import jax
import jax.numpy as jnp
from jax import lax

C = 64
SIDE = 16
LAYERS = 2
SITES = 256
SAMPLES = 512
N_SAMP = 32


def levels(rng, extent, shards, low, high):
    level, own = 1.0, jax.random.fold_in(rng, 6)
    for position, blocks in shards:
        heights = jnp.exp(jax.random.uniform(jax.random.fold_in(own, position), (blocks,), jnp.float32, low / len(shards), high / len(shards)))
        level = level * jnp.repeat(heights, extent[position] // blocks).reshape([-1 if axis == position else 1 for axis in range(len(extent))])
    return level


def setup_inputs(seed: int = 0) -> dict:
    splits = jax.random.split(jax.random.key(seed), 4)
    activations = jnp.clip(2.0 * jax.random.uniform(splits[0], (SAMPLES, LAYERS, C, SITES), jnp.float32) ** levels(splits[0], (SAMPLES, LAYERS, C, SITES), ((0, 32),), -0.2, 0.2), 0.0, 2.0).astype(jnp.bfloat16)
    cotangents = jnp.clip(-0.029907227 + 0.1295166 * jax.random.uniform(splits[1], (SAMPLES, LAYERS, C, SITES), jnp.float32) ** levels(splits[1], (SAMPLES, LAYERS, C, SITES), ((0, 32), (2, 16)), -0.2, 0.2), -0.029907227, 0.099609375).astype(jnp.bfloat16)
    energies = jnp.clip(-3.0 + 2.0 * jax.random.uniform(splits[2], (SAMPLES,), jnp.float32) ** levels(splits[2], (SAMPLES,), ((0, 32),), -0.2, 0.2), -3.0, -1.0)
    return dict(activations=activations, cotangents=cotangents, energies=energies)


reg_shift = 0.1

def block_grads(pair):
    acts, cots = pair
    sample_count = acts.shape[0]
    field = cots.astype(jnp.float32).reshape(sample_count, LAYERS, C, SIDE, SIDE)
    shifted = [jnp.roll(field, (row_step - 1, col_step - 1), axis=(3, 4)) for row_step in range(3) for col_step in range(3)]
    stacked = jnp.stack(shifted, axis=3).reshape(sample_count, LAYERS, C * 9, SIDE * SIDE)
    grads = jnp.einsum('slkx,slix->slki', stacked, acts.astype(jnp.float32), precision=lax.Precision.HIGHEST)
    grads = grads.reshape(sample_count, LAYERS, C, 9, C).transpose(0, 2, 1, 4, 3)
    return grads.reshape(sample_count, C * LAYERS * C * 9)

def reference(activations, cotangents, energies):
    total = activations.shape[0]
    params_all = LAYERS * C * C * 9
    acts = activations.reshape(N_SAMP, total // N_SAMP, LAYERS, C, SIDE * SIDE)
    cots = cotangents.reshape(N_SAMP, total // N_SAMP, LAYERS, C, SIDE * SIDE)
    grads = lax.map(block_grads, (acts, cots)).reshape(total, params_all)
    col_mean = lax.optimization_barrier(jnp.sum(grads, axis=0)) / total
    energy_mean = jnp.sum(energies) / total
    centered = ((grads - col_mean) * (1.0 / math.sqrt(params_all))).astype(jnp.bfloat16)
    deviation = energies - energy_mean
    gram = jnp.dot(centered.astype(jnp.float32), centered.T.astype(jnp.float32), preferred_element_type=jnp.float32)
    regular = gram + reg_shift * jnp.eye(total, dtype=jnp.float32)
    factor = jnp.linalg.cholesky(regular)
    forward = lax.linalg.triangular_solve(factor, deviation[:, None], left_side=True, lower=True)
    coeffs = lax.linalg.triangular_solve(factor, forward, left_side=True, lower=True, transpose_a=True)[:, 0]
    term = jnp.dot(coeffs[None, :], centered.astype(jnp.float32), precision=lax.Precision.HIGHEST)[0]
    update = -math.sqrt(params_all / total) * term
    return (update.reshape(C, LAYERS * C * 9), coeffs)
```

```python
import math

import jax
import jax.numpy as jnp
from jax import lax
from jax.experimental import pallas as pl
from jax.experimental.pallas import tpu as pltpu
from jax.sharding import PartitionSpec as P

C = 64
SIDE = 16
LAYERS = 2
SITES = SIDE * SIDE
OFFSETS = 9

N_Z, N_XH, N_CORE = 8, 2, 2
N_SAMP = N_Z * N_XH * N_CORE
N_XL, N_Y = 2, 8
N_PAR = N_XL * N_Y
N_X = N_XH * N_XL
OWN = 16
TOTAL = N_SAMP * OWN
OUT_OWN = C // N_PAR
LANES = LAYERS * C
ROWS = OFFSETS * OUT_OWN
EXTRA = ROWS - N_SAMP
PARAMS = LAYERS * C * C * OFFSETS
REG_SHIFT = 0.1

HALF = 640
PART = HALF + 8
PLANE = N_Z * N_Y
TILES = PART // 8
FIRST = 41
FLIP = FIRST + PLANE - 1
LOW = FLIP - (TILES - 1)
SPLIT = 8 * FIRST

MESH = pl.DeviceIdType.MESH
F32 = jnp.float32
BF16 = jnp.bfloat16


def remote(src, dst, send, recv, samp, par):
    return pltpu.make_async_remote_copy(
        src_ref=src,
        dst_ref=dst,
        send_sem=send,
        recv_sem=recv,
        device_id=(samp, par),
        device_id_type=MESH,
    )


def far_first(i):
    return (4 + ((i + 1) // 2) * (1 - 2 * (i % 2))) % 8


def whole_kernel(
    act_hbm, cot_hbm, en_ref, out_ref, coeff_ref,
    act_ref, cot_ref, fields, shifted, grads, land, own, chip, part, from_plane, from_x, fin,
    rows, row_land,
    act_sem, cot_sem, a2a_send, a2a_recv, ex_send, ex_recv, core_send, core_recv, cx_send, cx_recv, r_send, r_recv, rx_send,
    p_send, p_recv, x_send, x_recv, g_send, g_recv, s_send, s_recv, rx_recv, ready,
):
    samp = lax.axis_index("samp")
    par = lax.axis_index("par")
    z = samp // 4
    x_hi = (samp // 2) % 2
    core = samp % 2
    x_lo = par // N_Y
    y = par % N_Y
    x = x_hi * 2 + x_lo
    sibling = samp + 1 - 2 * core

    act_copy = pltpu.make_async_copy(act_hbm, act_ref, act_sem)
    act_copy.start()
    cot_copy = pltpu.make_async_copy(cot_hbm, cot_ref, cot_sem)
    cot_copy.start()

    def samp_peer(i):
        to_z = (z + far_first(i // 4)) % N_Z
        to_x = (x_hi + 1 - (i // 2) % 2) % 2
        return to_z * 4 + to_x * 2 + (core + 1 - i % 2) % 2

    def plane_peer(i):
        to_z = (z + far_first(i // 8)) % N_Z
        to_y = (y + far_first(i % 8)) % N_Y
        return to_z, to_y, to_z * 4 + samp % 4, x_lo * N_Y + to_y

    def x_peer(i):
        to = (x + 3 - i) % N_X
        return z * 4 + (to // 2) * 2 + core, (to % 2) * N_Y + y

    barrier = pltpu.get_barrier_semaphore()

    def greet(to_samp, to_par):
        pl.semaphore_signal(barrier, inc=1, device_id=(to_samp, to_par), device_id_type=MESH)

    def greet_samp(i, _):
        greet(samp_peer(i), par)
        return 0

    def y_peer(i):
        return x_lo * N_Y + (y + far_first(i)) % N_Y

    def greet_y(i, _):
        greet(samp, y_peer(i))
        return 0

    lax.fori_loop(0, N_SAMP - 1, greet_samp, 0)
    lax.fori_loop(0, N_Y - 1, greet_y, 0)
    greet(*x_peer(0))
    greet(*x_peer(2))

    cot_copy.wait()
    fields[:, 0:4, :] = cot_ref[:, 0].astype(F32)
    fields[:, 4:8, :] = cot_ref[:, 1].astype(F32)
    field = fields[...].reshape(OWN * 8, SITES)
    column = lax.broadcasted_iota(jnp.int32, field.shape, 1) % SIDE
    for b in (-1, 0, 1):
        if b == 1:
            moved = jnp.where(column == 0, pltpu.roll(field, SITES - 15, 1), pltpu.roll(field, 1, 1))
        elif b == -1:
            moved = jnp.where(column == 15, pltpu.roll(field, 15, 1), pltpu.roll(field, SITES - 1, 1))
        else:
            moved = field
        for a in (-1, 0, 1):
            k = 3 * (a + 1) + (b + 1)
            turned = moved if a == 0 else pltpu.roll(moved, (16 * a) % SITES, 1)
            shifted[:, 8 * k : 8 * k + 8, :] = turned.reshape(OWN, 8, SITES)

    act_copy.wait()
    first_layer = lax.broadcasted_iota(jnp.int32, (8, LANES), 1) < C

    def one_sample(s):
        product = lax.dot_general(
            shifted[s].astype(BF16), act_ref[s], (((1,), (1,)), ((), ())), preferred_element_type=F32
        )
        for k in range(OFFSETS):
            tile = product[8 * k : 8 * k + 8, :]
            mixed = jnp.where(first_layer, tile, pltpu.roll(tile, 4, 0))
            grads[pl.ds(4 * k * OWN + s, 4, stride=OWN), :] = mixed[:4]

    def some_samples(step, _):
        for i in range(4):
            one_sample(step * 4 + i)
        return 0

    lax.fori_loop(0, OWN // 4, some_samples, 0)

    pl.semaphore_wait(barrier, N_SAMP - 1 + N_Y - 1 + 2)

    def tell_y(i, _):
        pl.semaphore_signal(ready, inc=1, device_id=(samp, y_peer(i)), device_id_type=MESH)
        return 0

    lax.fori_loop(0, N_Y - 1, tell_y, 0)

    here = pl.multiple_of(samp * OWN, OWN)

    def group(r):
        return grads.at[pl.ds(pl.multiple_of(r * OWN, OWN), OWN)]

    def send_extra(j, _):
        @pl.when(samp != 8 * j)
        def _():
            remote(group(N_SAMP + j), land.at[1, pl.ds(here, OWN)], ex_send, ex_recv, 8 * j, par).start()

        return 0

    lax.fori_loop(0, EXTRA, send_extra, 0)

    def send_group(i, _):
        to = samp_peer(i)
        remote(group(to), land.at[0, pl.ds(here, OWN)], a2a_send, a2a_recv, to, par).start()
        return 0

    lax.fori_loop(0, N_SAMP - 1, send_group, 0)
    land[0, pl.ds(here, OWN), :] = grads[pl.ds(here, OWN), :]
    is_extra = samp % 8 == 0
    chip_extra = (samp // 2) % 4 == 0

    @pl.when(is_extra)
    def _():
        mine = pl.multiple_of((N_SAMP + samp // 8) * OWN, OWN)
        land[1, pl.ds(here, OWN), :] = grads[pl.ds(mine, OWN), :]

    @pl.when(jnp.logical_not(is_extra))
    def _():
        own[1] = jnp.zeros((TOTAL, LANES), BF16)

    @pl.when(jnp.logical_not(chip_extra))
    def _():
        chip[2] = jnp.zeros((TOTAL, LANES), BF16)

    row = lax.broadcasted_iota(jnp.int32, (8, LANES), 0)
    lane = lax.broadcasted_iota(jnp.int32, (8, LANES), 1)
    own_place = (row == samp // 8) & (lane // OWN == samp % 8) & (par == 0)
    part[HALF:PART, :] = jnp.where(own_place, jnp.broadcast_to(en_ref[...], (8, LANES)), 0.0)

    def wait_recv(ref, sem):
        remote(ref, ref, a2a_send, sem, samp, par).wait_recv()

    def wait_send(ref, sem):
        remote(ref, ref, sem, a2a_recv, samp, par).wait_send()

    most = (N_SAMP - 1) * OWN

    def centre(slot):
        block = land[slot]
        mean = jnp.sum(block, axis=0, keepdims=True) / TOTAL
        return ((block - mean) * (1.0 / math.sqrt(PARAMS))).astype(BF16)

    wait_recv(land.at[0, pl.ds(0, most)], a2a_recv)
    c0 = centre(0)
    own[0] = c0
    chip[core] = c0
    remote(chip.at[core], chip.at[core], core_send, core_recv, sibling, par).start()

    @pl.when(is_extra)
    def _():
        wait_recv(land.at[1, pl.ds(0, most)], ex_recv)
        c = centre(1)
        own[1] = c
        chip[2] = c
        remote(chip.at[2], chip.at[2], cx_send, cx_recv, sibling, par).start()

    @pl.when(chip_extra & (core == 1))
    def _():
        wait_recv(chip.at[2], cx_recv)

    wait_recv(chip.at[1 - core], core_recv)

    def gram_block(i, _):
        n = core * 5 + i
        a = n % 4
        b = (a + n // 4) % 4
        total = jnp.zeros((128, 128), F32)
        for q in range(3):
            left = chip[q, pl.ds(pl.multiple_of(a * 128, 128), 128), :]
            right = chip[q, pl.ds(pl.multiple_of(b * 128, 128), 128), :]
            total += lax.dot_general(left, right, (((1,), (1,)), ((), ())), preferred_element_type=F32)
        part[pl.ds(pl.multiple_of(i * 128, 128), 128), :] = total
        return 0

    lax.fori_loop(0, 5, gram_block, 0)

    pl.semaphore_wait(ready, N_Y - 1)

    def place(at_z, at_y):
        return ((at_z * N_Y + at_y) * 13) % PLANE

    me = place(z, y)

    def tile(t):
        return pl.ds(pl.multiple_of(8 * t, 8), 8)

    def reduces(batch, q):
        return q < FIRST if batch == 0 else q >= LOW

    def tile_of(batch, q):
        return jnp.minimum(q, FIRST - 1) if batch == 0 else FLIP - jnp.maximum(q, LOW)

    def send_part(batch):
        def body(i, _):
            to_z, to_y, to_samp, to_par = plane_peer(i)
            q = place(to_z, to_y)

            @pl.when(reduces(batch, q))
            def _():
                remote(
                    part.at[tile(tile_of(batch, q))], from_plane.at[batch, me],
                    p_send.at[batch], p_recv.at[batch], to_samp, to_par,
                ).start()

            return 0

        lax.fori_loop(0, PLANE - 1, body, 0)

    def reduce_plane(batch):
        @pl.when(reduces(batch, me))
        def _():
            from_plane[batch, me] = part[tile(tile_of(batch, me)), :]
            wait_recv(from_plane.at[batch, pl.ds(0, PLANE - 1)], p_recv.at[batch])
            from_x[batch, x] = jnp.sum(from_plane[batch], axis=0)

            def send_x(i, _):
                to_samp, to_par = x_peer(i)
                mine = from_x.at[batch, x]
                remote(mine, mine, x_send.at[batch], x_recv.at[batch], to_samp, to_par).start()
                return 0

            lax.fori_loop(0, N_X - 1, send_x, 0)

    def spread_sum(batch):
        @pl.when(reduces(batch, me))
        def _():
            wait_recv(from_x.at[batch, pl.ds(0, N_X - 1)], x_recv.at[batch])
            mine = fin.at[core, tile(tile_of(batch, me))]
            fin[core, tile(tile_of(batch, me)), :] = jnp.sum(from_x[batch], axis=0)

            def send_sum(i, _):
                _, _, to_samp, to_par = plane_peer(i)
                remote(mine, mine, g_send.at[batch], g_recv.at[batch], to_samp, to_par).start()
                return 0

            lax.fori_loop(0, PLANE - 1, send_sum, 0)

    spans = ((0, SPLIT), (SPLIT, PART - SPLIT))

    def span(batch):
        start, size = spans[batch]
        return pl.ds(start, size)

    def gathered(batch):
        start, size = spans[batch]

        @pl.when(reduces(batch, me))
        def _():
            wait_recv(fin.at[core, pl.ds(start, size - 8)], g_recv.at[batch])

        @pl.when(jnp.logical_not(reduces(batch, me)))
        def _():
            wait_recv(fin.at[core, pl.ds(start, size)], g_recv.at[batch])

        remote(
            fin.at[core, span(batch)], fin.at[core, span(batch)], s_send.at[batch], s_recv.at[batch], sibling, par
        ).start()

    def complete(batch):
        wait_recv(fin.at[1 - core, span(batch)], s_recv.at[batch])

    send_part(0)
    send_part(1)
    reduce_plane(0)
    reduce_plane(1)
    spread_sum(0)
    spread_sum(1)
    gathered(0)
    complete(0)
    diag = fin[0, 0:128, :] + shift_matrix()
    first = jnp.concatenate(invert([diag[8 * q : 8 * q + 8, :] for q in range(16)]), axis=0)
    gathered(1)
    complete(1)

    solve(first, fin, own, coeff_ref, rows, samp)

    extra = N_SAMP + samp // 8

    @pl.when(is_extra)
    def _():
        def send_second(i, _):
            remote(rows.at[1, pl.ds(0, 1)], row_land.at[extra, pl.ds(0, 1)], rx_send, rx_recv.at[samp // 8], samp_peer(i), par).start()
            return 0

        lax.fori_loop(0, N_SAMP - 1, send_second, 0)
        row_land[extra] = rows[1]

    def send_row(i, _):
        remote(rows.at[0, pl.ds(0, 1)], row_land.at[samp, pl.ds(0, 1)], r_send, r_recv, samp_peer(i), par).start()
        return 0

    lax.fori_loop(0, N_SAMP - 1, send_row, 0)
    row_land[samp] = rows[0]

    wait_send(land.at[0, pl.ds(0, most)], a2a_send)

    def sent_extra(j, _):
        @pl.when(samp != 8 * j)
        def _():
            wait_send(land.at[1, pl.ds(0, OWN)], ex_send)

        return 0

    lax.fori_loop(0, EXTRA, sent_extra, 0)
    wait_send(chip.at[core], core_send)

    @pl.when(is_extra)
    def _():
        wait_send(chip.at[2], cx_send)

    for batch in range(2):

        @pl.when(reduces(batch, me))
        def _():
            wait_send(part.at[pl.ds(0, spans[batch][1] - 8)], p_send.at[batch])
            wait_send(from_x.at[batch, pl.ds(0, N_X - 1)], x_send.at[batch])
            wait_send(from_plane.at[batch, pl.ds(0, PLANE - 1)], g_send.at[batch])

        @pl.when(jnp.logical_not(reduces(batch, me)))
        def _():
            wait_send(part.at[pl.ds(0, spans[batch][1])], p_send.at[batch])

        wait_send(fin.at[core, span(batch)], s_send.at[batch])

    others = row_land.at[pl.ds(0, N_SAMP - 1), pl.ds(0, 1)]
    wait_recv(others, r_recv)

    def await_extra(j, _):
        @pl.when(samp != 8 * j)
        def _():
            wait_recv(row_land.at[0, pl.ds(0, 1)], rx_recv.at[j])

        return 0

    lax.fori_loop(0, EXTRA, await_extra, 0)
    out_ref[...] = row_land[:, 0, :]
    wait_send(others, r_send)

    @pl.when(is_extra)
    def _():
        wait_send(others, rx_send)


def whole(act, cot, energies):
    dma = pltpu.SemaphoreType.DMA
    vmem = pl.BlockSpec(memory_space=pltpu.VMEM)
    hbm = pl.BlockSpec(memory_space=pltpu.HBM)
    return pl.pallas_call(
        whole_kernel,
        out_shape=(
            jax.ShapeDtypeStruct((ROWS, LANES), F32),
            jax.ShapeDtypeStruct((1, OWN), F32),
        ),
        in_specs=[hbm, hbm, vmem],
        out_specs=(vmem, vmem),
        scratch_shapes=[
            pltpu.VMEM((OWN, LANES, SITES), BF16),
            pltpu.VMEM((OWN, LAYERS, OUT_OWN, SITES), BF16),
            pltpu.VMEM((OWN, 8, SITES), F32),
            pltpu.VMEM((OWN, 8 * OFFSETS, SITES), F32),
            pltpu.VMEM((ROWS * OWN, LANES), F32),
            pltpu.VMEM((2, TOTAL, LANES), F32),
            pltpu.VMEM((2, TOTAL, LANES), BF16),
            pltpu.VMEM((3, TOTAL, LANES), BF16),
            pltpu.VMEM((PART, LANES), F32),
            pltpu.VMEM((2, PLANE, 8, LANES), F32),
            pltpu.VMEM((2, N_X, 8, LANES), F32),
            pltpu.VMEM((N_CORE, PART, LANES), F32),
            pltpu.VMEM((2, 8, 128), F32),
            pltpu.VMEM((ROWS, 8, LANES), F32),
        ]
        + [dma] * 13
        + [dma((2,))] * 8
        + [dma((EXTRA,)), pltpu.SemaphoreType.REGULAR],
        compiler_params=pltpu.CompilerParams(
            collective_id=0, has_side_effects=True, vmem_limit_bytes=60 * 2**20
        ),
    )(act, cot, energies)


def dot(left, right, dims):
    return lax.dot_general(
        left, right, (dims, ((), ())), precision=lax.Precision.HIGHEST, preferred_element_type=F32
    )


def tree_sum(terms):
    while len(terms) > 1:
        paired = [terms[i] + terms[i + 1] for i in range(0, len(terms) - 1, 2)]
        terms = paired + terms[2 * len(paired) :]
    return terms[0]


def invert(tiles):
    tiles = list(tiles)
    lane = lax.broadcasted_iota(jnp.int32, (8, 128), 1)
    sub = lax.broadcasted_iota(jnp.int32, (8, 128), 0)
    on = [sub == r for r in range(8)]
    zero = jnp.zeros((8, 128), F32)

    def along_lanes(v, j):
        return jnp.broadcast_to(v[:, j : j + 1], (8, 128))

    def along_rows(v, j):
        return jnp.broadcast_to(v[j : j + 1, :], (8, 128))

    for p in range(8):
        base = 16 * p
        inside = (lane >= base) & (lane < base + 16)
        pivot_rows = tiles[2 * p : 2 * p + 2]
        cols = [[along_lanes(v, base + m) for m in range(16)] for v in pivot_rows]
        work = [
            jnp.where(inside, jnp.where(lane - base - 8 * t == sub, 1.0, 0.0), v) for t, v in enumerate(pivot_rows)
        ]
        for j in range(16):
            h, r = divmod(j, 8)
            inverse = 1.0 / along_rows(cols[h][j], r)

            def sweep(pair):
                turned = along_rows(pair[h], r) * inverse
                new = [pair[t] - cols[t][j] * turned for t in range(2)]
                new[h] = jnp.where(on[r], turned, new[h])
                return new

            for m in range(j + 1, 16):
                cols[0][m], cols[1][m] = sweep((cols[0][m], cols[1][m]))
            work = sweep(work)
        spread = [along_rows(work[j // 8], j % 8) for j in range(16)]
        near = [2 * p + 2, 2 * p + 3] if p < 7 else []
        rest = [q for q in range(16) if q not in near and q // 2 != p]
        new = {}
        for q in near:
            new[q] = jnp.where(inside, 0.0, tiles[q]) - tree_sum(
                [along_lanes(tiles[q], base + j) * spread[j] for j in range(16)]
            )
        left = jnp.concatenate([tiles[q] for q in rest], axis=0)
        right = jnp.concatenate([work[q - 2 * p] if q // 2 == p else zero for q in range(16)], axis=0)
        product = dot(left, right, ((1,), (0,)))
        for i, q in enumerate(rest):
            new[q] = jnp.where(inside, 0.0, tiles[q]) - product[8 * i : 8 * i + 8]
        for q in new:
            tiles[q] = new[q]
        tiles[2 * p : 2 * p + 2] = work
    return tiles


def shift_matrix():
    return jnp.where(
        lax.broadcasted_iota(jnp.int32, (128, 128), 0) == lax.broadcasted_iota(jnp.int32, (128, 128), 1),
        REG_SHIFT, 0.0,
    ).astype(F32)


def solve(first, fin, own, coeff_ref, rows, samp):
    B = 128
    blocks = {}
    for n in range(10):
        a = n % 4
        b = (a + n // 4) % 4
        core, i = divmod(n, 5)
        value = fin[core, B * i : B * i + B, :]
        if a == b:
            value = value + shift_matrix()
        if a > b:
            a, b, value = b, a, value.T
        blocks[a, b] = value

    energies = fin[0, HALF:PART, :] + fin[1, HALF:PART, :]
    mean = jnp.sum(energies, axis=(0, 1), keepdims=True) / TOTAL
    rhs = [jnp.broadcast_to(energies[a : a + 1, :] - mean, (8, B)) for a in range(4)]

    upper = {}
    for s in range(4):
        if s == 0:
            p = first
        else:
            p = jnp.concatenate(invert([blocks[s, s][8 * q : 8 * q + 8] for q in range(16)]), axis=0)
        for j in range(s + 1, 4):
            upper[s, j] = dot(p, blocks[s, j], ((1,), (0,)))
        for i in range(s + 1, 4):
            for j in range(i, 4):
                blocks[i, j] = blocks[i, j] - dot(blocks[s, i], upper[s, j], ((0,), (0,)))
        u = dot(rhs[s], p, ((1,), (0,)))
        for j in range(s + 1, 4):
            rhs[j] = rhs[j] - dot(u, blocks[s, j], ((1,), (0,)))
        rhs[s] = u
    for s in (2, 1, 0):
        for j in range(s + 1, 4):
            rhs[s] = rhs[s] - dot(rhs[j], upper[s, j], ((1,), (1,)))

    scale = -math.sqrt(PARAMS / TOTAL)
    mine = rhs[0]
    for a in range(1, 4):
        mine = jnp.where(samp // 8 == a, rhs[a], mine)
    coeff_ref[...] = pltpu.roll(mine, (128 - OWN * (samp % 8)) % 128, 1)[0:1, 0:OWN]
    for slot in range(2):
        total = jnp.zeros((8, B), F32)
        for a in range(4):
            total += dot(rhs[a], own[slot, B * a : B * a + B, :].astype(F32), ((1,), (0,)))
        rows[slot] = scale * total


def local(activations, cotangents, energies):
    act = activations.reshape(OWN, LANES, SITES)
    spread = jnp.tile(energies, 128 // OWN).reshape(1, LANES)
    rows, coeffs = whole(act, cotangents, spread)
    update = rows.reshape(OFFSETS, OUT_OWN, LANES).transpose(1, 2, 0).reshape(OUT_OWN, -1)
    return update, coeffs.reshape(OWN)


def solution(mesh):
    return jax.shard_map(
        local,
        mesh=mesh,
        in_specs=(P("samp", None, None, None), P("samp", None, "par", None), P("samp")),
        out_specs=(P("par", None), P("samp")),
        check_vma=False,
    )
```

```python
import math

import jax
import jax.numpy as jnp
from jax import lax
from jax.experimental import pallas as pl
from jax.experimental.pallas import tpu as pltpu
from jax.sharding import PartitionSpec as P

C = 64
SIDE = 16
LAYERS = 2
SITES = SIDE * SIDE
OFFSETS = 9

N_Z, N_XH, N_CORE = 8, 2, 2
N_SAMP = N_Z * N_XH * N_CORE
N_XL, N_Y = 2, 8
N_PAR = N_XL * N_Y
N_X = N_XH * N_XL
OWN = 16
TOTAL = N_SAMP * OWN
OUT_OWN = C // N_PAR
LANES = LAYERS * C
ROWS = OFFSETS * OUT_OWN
EXTRA = ROWS - N_SAMP
PARAMS = LAYERS * C * C * OFFSETS
REG_SHIFT = 0.1

HALF = 640
PART = HALF + 8
PLANE = N_Z * N_Y
TILES = PART // 8
FIRST = 41
FLIP = FIRST + PLANE - 1
LOW = FLIP - (TILES - 1)
SPLIT = 8 * FIRST

MESH = pl.DeviceIdType.MESH
F32 = jnp.float32
BF16 = jnp.bfloat16


def remote(src, dst, send, recv, samp, par):
    return pltpu.make_async_remote_copy(
        src_ref=src,
        dst_ref=dst,
        send_sem=send,
        recv_sem=recv,
        device_id=(samp, par),
        device_id_type=MESH,
    )


def far_first(i):
    return (4 + ((i + 1) // 2) * (1 - 2 * (i % 2))) % 8


def whole_kernel(
    act_hbm, cot_hbm, en_hbm, out_ref, coeff_ref,
    act_ref, cot_ref, en_ref, spot, fields, shifted, grads, land, own, chip, part, from_plane, from_x, fin,
    rows, row_land,
    act_sem, cot_sem, en_sem, a2a_send, a2a_recv, ex_send, ex_recv, core_send, core_recv, cx_send, cx_recv, r_send, r_recv, rx_send,
    p_send, p_recv, x_send, x_recv, g_send, g_recv, s_send, s_recv, rx_recv, ready,
):
    samp = lax.axis_index("samp")
    par = lax.axis_index("par")
    z = samp // 4
    x_hi = (samp // 2) % 2
    core = samp % 2
    x_lo = par // N_Y
    y = par % N_Y
    x = x_hi * 2 + x_lo
    sibling = samp + 1 - 2 * core

    act_copy = pltpu.make_async_copy(act_hbm, act_ref, act_sem)
    act_copy.start()
    cot_copy = pltpu.make_async_copy(cot_hbm, cot_ref, cot_sem)
    cot_copy.start()
    en_copy = pltpu.make_async_copy(en_hbm, en_ref, en_sem)
    en_copy.start()

    def samp_peer(i):
        to_z = (z + far_first(i // 4)) % N_Z
        to_x = (x_hi + 1 - (i // 2) % 2) % 2
        return to_z * 4 + to_x * 2 + (core + 1 - i % 2) % 2

    def plane_peer(i):
        to_z = (z + far_first(i // 8)) % N_Z
        to_y = (y + far_first(i % 8)) % N_Y
        return to_z, to_y, to_z * 4 + samp % 4, x_lo * N_Y + to_y

    def x_peer(i):
        to = (x + 3 - i) % N_X
        return z * 4 + (to // 2) * 2 + core, (to % 2) * N_Y + y

    barrier = pltpu.get_barrier_semaphore()

    def greet(to_samp, to_par):
        pl.semaphore_signal(barrier, inc=1, device_id=(to_samp, to_par), device_id_type=MESH)

    def greet_samp(i, _):
        greet(samp_peer(i), par)
        return 0

    def y_peer(i):
        return x_lo * N_Y + (y + far_first(i)) % N_Y

    def greet_y(i, _):
        greet(samp, y_peer(i))
        return 0

    lax.fori_loop(0, N_SAMP - 1, greet_samp, 0)
    lax.fori_loop(0, N_Y - 1, greet_y, 0)
    greet(*x_peer(0))
    greet(*x_peer(2))

    cot_copy.wait()
    fields[:, 0:4, :] = cot_ref[:, 0].astype(F32)
    fields[:, 4:8, :] = cot_ref[:, 1].astype(F32)
    field = fields[...].reshape(OWN * 8, SITES)
    column = lax.broadcasted_iota(jnp.int32, field.shape, 1) % SIDE
    for b in (-1, 0, 1):
        if b == 1:
            moved = jnp.where(column == 0, pltpu.roll(field, SITES - 15, 1), pltpu.roll(field, 1, 1))
        elif b == -1:
            moved = jnp.where(column == 15, pltpu.roll(field, 15, 1), pltpu.roll(field, SITES - 1, 1))
        else:
            moved = field
        for a in (-1, 0, 1):
            k = 3 * (a + 1) + (b + 1)
            turned = moved if a == 0 else pltpu.roll(moved, (16 * a) % SITES, 1)
            shifted[:, 8 * k : 8 * k + 8, :] = turned.reshape(OWN, 8, SITES)

    act_copy.wait()
    en_copy.wait()
    first_layer = lax.broadcasted_iota(jnp.int32, (8, LANES), 1) < C

    half = OWN // 2

    def one_sample(part_no, i):
        s = part_no * half + i
        product = lax.dot_general(
            shifted[s].astype(BF16), act_ref[s], (((1,), (1,)), ((), ())), preferred_element_type=F32
        )
        for k in range(OFFSETS):
            tile = product[8 * k : 8 * k + 8, :]
            mixed = jnp.where(first_layer, tile, pltpu.roll(tile, 4, 0))
            grads[part_no, pl.ds(4 * k * half + i, 4, stride=half), :] = mixed[:4]

    def some_samples(part_no):
        def body(step, _):
            for i in range(4):
                one_sample(part_no, step * 4 + i)
            return 0

        lax.fori_loop(0, half // 4, body, 0)

    here = pl.multiple_of(samp * OWN, OWN)

    def send_groups(part_no):
        there = pl.ds(pl.multiple_of(here + part_no * half, half), half)

        def group(r):
            return grads.at[part_no, pl.ds(pl.multiple_of(r * half, half), half)]

        def send_extra(j, _):
            @pl.when(samp != 8 * j)
            def _():
                remote(group(N_SAMP + j), land.at[1, there], ex_send, ex_recv, 8 * j, par).start()

            return 0

        lax.fori_loop(0, EXTRA, send_extra, 0)

        def send_group(i, _):
            to = samp_peer(i)
            remote(group(to), land.at[0, there], a2a_send, a2a_recv, to, par).start()
            return 0

        lax.fori_loop(0, N_SAMP - 1, send_group, 0)

    some_samples(0)
    pl.semaphore_wait(barrier, N_SAMP - 1 + N_Y - 1 + 2)

    def tell_y(i, _):
        pl.semaphore_signal(ready, inc=1, device_id=(samp, y_peer(i)), device_id_type=MESH)
        return 0

    lax.fori_loop(0, N_Y - 1, tell_y, 0)

    send_groups(0)
    some_samples(1)
    send_groups(1)

    def keep(slot, r):
        for part_no in range(2):
            there = pl.ds(pl.multiple_of(here + part_no * half, half), half)
            land[slot, there, :] = grads[part_no, pl.ds(pl.multiple_of(r * half, half), half), :]

    keep(0, samp)
    is_extra = samp % 8 == 0
    chip_extra = (samp // 2) % 4 == 0

    @pl.when(is_extra)
    def _():
        keep(1, N_SAMP + samp // 8)

    @pl.when(jnp.logical_not(is_extra))
    def _():
        own[1] = jnp.zeros((TOTAL, LANES), BF16)

    @pl.when(jnp.logical_not(chip_extra))
    def _():
        chip[2] = jnp.zeros((TOTAL, LANES), BF16)

    row = lax.broadcasted_iota(jnp.int32, (8, LANES), 0)
    lane = lax.broadcasted_iota(jnp.int32, (8, LANES), 1)
    own_place = (row == samp // 8) & (lane // OWN == samp % 8) & (par == 0)
    spot[...] = jnp.zeros((8, LANES), F32)
    spot[0:1, 0:OWN] = en_ref[...]
    moved = pltpu.roll(spot[...], OWN * (samp % 8), 1)
    part[HALF:PART, :] = jnp.where(own_place, jnp.broadcast_to(moved[0:1, :], (8, LANES)), 0.0)

    def wait_recv(ref, sem):
        remote(ref, ref, a2a_send, sem, samp, par).wait_recv()

    def wait_send(ref, sem):
        remote(ref, ref, sem, a2a_recv, samp, par).wait_send()

    most = (N_SAMP - 1) * OWN

    def centre(slot):
        block = land[slot]
        mean = jnp.sum(block, axis=0, keepdims=True) / TOTAL
        return ((block - mean) * (1.0 / math.sqrt(PARAMS))).astype(BF16)

    @pl.when(is_extra)
    def _():
        wait_recv(land.at[1, pl.ds(0, most)], ex_recv)
        c = centre(1)
        own[1] = c
        chip[2] = c
        remote(chip.at[2], chip.at[2], cx_send, cx_recv, sibling, par).start()

    wait_recv(land.at[0, pl.ds(0, most)], a2a_recv)
    c0 = centre(0)
    own[0] = c0
    chip[core] = c0
    remote(chip.at[core], chip.at[core], core_send, core_recv, sibling, par).start()

    @pl.when(chip_extra & (core == 1))
    def _():
        wait_recv(chip.at[2], cx_recv)

    wait_recv(chip.at[1 - core], core_recv)

    def gram_block(i):
        n = core * 5 + i
        a = n % 4
        b = (a + n // 4) % 4
        total = jnp.zeros((128, 128), F32)
        for q in range(3):
            left = chip[q, pl.ds(pl.multiple_of(a * 128, 128), 128), :]
            right = chip[q, pl.ds(pl.multiple_of(b * 128, 128), 128), :]
            total += lax.dot_general(left, right, (((1,), (1,)), ((), ())), preferred_element_type=F32)
        part[128 * i : 128 * i + 128, :] = total

    pl.semaphore_wait(ready, N_Y - 1)

    def place(at_z, at_y):
        return ((at_z * N_Y + at_y) * 13) % PLANE

    me = place(z, y)

    def tile(t):
        return pl.ds(pl.multiple_of(8 * t, 8), 8)

    def reduces(batch, q):
        return q < FIRST if batch == 0 else q >= LOW

    def tile_of(batch, q):
        return jnp.minimum(q, FIRST - 1) if batch == 0 else FLIP - jnp.maximum(q, LOW)

    def send_part(batch):
        def body(i, _):
            to_z, to_y, to_samp, to_par = plane_peer(i)
            q = place(to_z, to_y)

            @pl.when(reduces(batch, q))
            def _():
                remote(
                    part.at[tile(tile_of(batch, q))], from_plane.at[batch, me],
                    p_send.at[batch], p_recv.at[batch], to_samp, to_par,
                ).start()

            return 0

        lax.fori_loop(0, PLANE - 1, body, 0)

    def reduce_plane(batch):
        @pl.when(reduces(batch, me))
        def _():
            from_plane[batch, me] = part[tile(tile_of(batch, me)), :]
            wait_recv(from_plane.at[batch, pl.ds(0, PLANE - 1)], p_recv.at[batch])
            from_x[batch, x] = jnp.sum(from_plane[batch], axis=0)

            def send_x(i, _):
                to_samp, to_par = x_peer(i)
                mine = from_x.at[batch, x]
                remote(mine, mine, x_send.at[batch], x_recv.at[batch], to_samp, to_par).start()
                return 0

            lax.fori_loop(0, N_X - 1, send_x, 0)

    def spread_sum(batch):
        @pl.when(reduces(batch, me))
        def _():
            wait_recv(from_x.at[batch, pl.ds(0, N_X - 1)], x_recv.at[batch])
            mine = fin.at[core, tile(tile_of(batch, me))]
            fin[core, tile(tile_of(batch, me)), :] = jnp.sum(from_x[batch], axis=0)

            def send_sum(i, _):
                _, _, to_samp, to_par = plane_peer(i)
                remote(mine, mine, g_send.at[batch], g_recv.at[batch], to_samp, to_par).start()
                return 0

            lax.fori_loop(0, PLANE - 1, send_sum, 0)

    spans = ((0, SPLIT), (SPLIT, PART - SPLIT))

    def span(batch):
        start, size = spans[batch]
        return pl.ds(start, size)

    def gathered(batch):
        start, size = spans[batch]

        @pl.when(reduces(batch, me))
        def _():
            wait_recv(fin.at[core, pl.ds(start, size - 8)], g_recv.at[batch])

        @pl.when(jnp.logical_not(reduces(batch, me)))
        def _():
            wait_recv(fin.at[core, pl.ds(start, size)], g_recv.at[batch])

        remote(
            fin.at[core, span(batch)], fin.at[core, span(batch)], s_send.at[batch], s_recv.at[batch], sibling, par
        ).start()

    def complete(batch):
        wait_recv(fin.at[1 - core, span(batch)], s_recv.at[batch])

    for i in range(3):
        gram_block(i)
    send_part(0)
    for i in range(3, 5):
        gram_block(i)
    send_part(1)
    reduce_plane(0)
    reduce_plane(1)
    spread_sum(0)
    spread_sum(1)
    gathered(0)
    complete(0)
    diag = fin[0, 0:128, :] + shift_matrix()
    first = jnp.concatenate(invert([diag[8 * q : 8 * q + 8, :] for q in range(16)]), axis=0)
    gathered(1)
    complete(1)

    solve(first, fin, own, coeff_ref, rows, samp)

    extra = N_SAMP + samp // 8

    @pl.when(is_extra)
    def _():
        def send_second(i, _):
            remote(rows.at[1, pl.ds(0, 1)], row_land.at[extra, pl.ds(0, 1)], rx_send, rx_recv.at[samp // 8], samp_peer(i), par).start()
            return 0

        lax.fori_loop(0, N_SAMP - 1, send_second, 0)
        row_land[extra] = rows[1]

    def send_row(i, _):
        remote(rows.at[0, pl.ds(0, 1)], row_land.at[samp, pl.ds(0, 1)], r_send, r_recv, samp_peer(i), par).start()
        return 0

    lax.fori_loop(0, N_SAMP - 1, send_row, 0)
    row_land[samp] = rows[0]

    wait_send(land.at[0, pl.ds(0, most)], a2a_send)

    def sent_extra(j, _):
        @pl.when(samp != 8 * j)
        def _():
            wait_send(land.at[1, pl.ds(0, OWN)], ex_send)

        return 0

    lax.fori_loop(0, EXTRA, sent_extra, 0)
    wait_send(chip.at[core], core_send)

    @pl.when(is_extra)
    def _():
        wait_send(chip.at[2], cx_send)

    for batch in range(2):

        @pl.when(reduces(batch, me))
        def _():
            wait_send(part.at[pl.ds(0, spans[batch][1] - 8)], p_send.at[batch])
            wait_send(from_x.at[batch, pl.ds(0, N_X - 1)], x_send.at[batch])
            wait_send(from_plane.at[batch, pl.ds(0, PLANE - 1)], g_send.at[batch])

        @pl.when(jnp.logical_not(reduces(batch, me)))
        def _():
            wait_send(part.at[pl.ds(0, spans[batch][1])], p_send.at[batch])

        wait_send(fin.at[core, span(batch)], s_send.at[batch])

    others = row_land.at[pl.ds(0, N_SAMP - 1), pl.ds(0, 1)]
    wait_recv(others, r_recv)

    def await_extra(j, _):
        @pl.when(samp != 8 * j)
        def _():
            wait_recv(row_land.at[0, pl.ds(0, 1)], rx_recv.at[j])

        return 0

    lax.fori_loop(0, EXTRA, await_extra, 0)
    for o in range(OUT_OWN):
        taken = [row_land[k * OUT_OWN + o, 0:1, :] for k in range(OFFSETS)]
        taken.append(jnp.zeros((16 - OFFSETS, LANES), F32))
        out_ref[o] = jnp.concatenate(taken, axis=0).T[:, 0:OFFSETS]
    wait_send(others, r_send)

    @pl.when(is_extra)
    def _():
        wait_send(others, rx_send)


def whole(act, cot, energies):
    dma = pltpu.SemaphoreType.DMA
    vmem = pl.BlockSpec(memory_space=pltpu.VMEM)
    hbm = pl.BlockSpec(memory_space=pltpu.HBM)
    return pl.pallas_call(
        whole_kernel,
        out_shape=(
            jax.ShapeDtypeStruct((OUT_OWN, LANES, OFFSETS), F32),
            jax.ShapeDtypeStruct((1, OWN), F32),
        ),
        in_specs=[hbm, hbm, hbm],
        out_specs=(vmem, vmem),
        scratch_shapes=[
            pltpu.VMEM((OWN, LANES, SITES), BF16),
            pltpu.VMEM((OWN, LAYERS, OUT_OWN, SITES), BF16),
            pltpu.VMEM((1, OWN), F32),
            pltpu.VMEM((8, LANES), F32),
            pltpu.VMEM((OWN, 8, SITES), F32),
            pltpu.VMEM((OWN, 8 * OFFSETS, SITES), F32),
            pltpu.VMEM((2, ROWS * OWN // 2, LANES), F32),
            pltpu.VMEM((2, TOTAL, LANES), F32),
            pltpu.VMEM((2, TOTAL, LANES), BF16),
            pltpu.VMEM((3, TOTAL, LANES), BF16),
            pltpu.VMEM((PART, LANES), F32),
            pltpu.VMEM((2, PLANE, 8, LANES), F32),
            pltpu.VMEM((2, N_X, 8, LANES), F32),
            pltpu.VMEM((N_CORE, PART, LANES), F32),
            pltpu.VMEM((2, 8, 128), F32),
            pltpu.VMEM((ROWS, 8, LANES), F32),
        ]
        + [dma] * 14
        + [dma((2,))] * 8
        + [dma((EXTRA,)), pltpu.SemaphoreType.REGULAR],
        compiler_params=pltpu.CompilerParams(
            collective_id=0, has_side_effects=True, vmem_limit_bytes=60 * 2**20
        ),
    )(act, cot, energies)


def dot(left, right, dims):
    return lax.dot_general(
        left, right, (dims, ((), ())), precision=lax.Precision.HIGHEST, preferred_element_type=F32
    )


def tree_sum(terms):
    while len(terms) > 1:
        paired = [terms[i] + terms[i + 1] for i in range(0, len(terms) - 1, 2)]
        terms = paired + terms[2 * len(paired) :]
    return terms[0]


def invert(tiles):
    tiles = list(tiles)
    lane = lax.broadcasted_iota(jnp.int32, (8, 128), 1)
    sub = lax.broadcasted_iota(jnp.int32, (8, 128), 0)
    on = [sub == r for r in range(8)]
    zero = jnp.zeros((8, 128), F32)

    def along_lanes(v, j):
        return jnp.broadcast_to(v[:, j : j + 1], (8, 128))

    def along_rows(v, j):
        return jnp.broadcast_to(v[j : j + 1, :], (8, 128))

    for p in range(8):
        base = 16 * p
        inside = (lane >= base) & (lane < base + 16)
        pivot_rows = tiles[2 * p : 2 * p + 2]
        cols = [[along_lanes(v, base + m) for m in range(16)] for v in pivot_rows]
        work = [
            jnp.where(inside, jnp.where(lane - base - 8 * t == sub, 1.0, 0.0), v) for t, v in enumerate(pivot_rows)
        ]
        for j in range(16):
            h, r = divmod(j, 8)
            inverse = 1.0 / along_rows(cols[h][j], r)

            def sweep(pair):
                turned = along_rows(pair[h], r) * inverse
                new = [pair[t] - cols[t][j] * turned for t in range(2)]
                new[h] = jnp.where(on[r], turned, new[h])
                return new

            for m in range(j + 1, 16):
                cols[0][m], cols[1][m] = sweep((cols[0][m], cols[1][m]))
            work = sweep(work)
        spread = [along_rows(work[j // 8], j % 8) for j in range(16)]
        near = [2 * p + 2, 2 * p + 3] if p < 7 else []
        rest = [q for q in range(16) if q not in near and q // 2 != p]
        new = {}
        for q in near:
            new[q] = jnp.where(inside, 0.0, tiles[q]) - tree_sum(
                [along_lanes(tiles[q], base + j) * spread[j] for j in range(16)]
            )
        left = jnp.concatenate([tiles[q] for q in rest], axis=0)
        right = jnp.concatenate([work[q - 2 * p] if q // 2 == p else zero for q in range(16)], axis=0)
        product = dot(left, right, ((1,), (0,)))
        for i, q in enumerate(rest):
            new[q] = jnp.where(inside, 0.0, tiles[q]) - product[8 * i : 8 * i + 8]
        for q in new:
            tiles[q] = new[q]
        tiles[2 * p : 2 * p + 2] = work
    return tiles


def shift_matrix():
    return jnp.where(
        lax.broadcasted_iota(jnp.int32, (128, 128), 0) == lax.broadcasted_iota(jnp.int32, (128, 128), 1),
        REG_SHIFT, 0.0,
    ).astype(F32)


def solve(first, fin, own, coeff_ref, rows, samp):
    B = 128
    blocks = {}
    for n in range(10):
        a = n % 4
        b = (a + n // 4) % 4
        core, i = divmod(n, 5)
        value = fin[core, B * i : B * i + B, :]
        if a == b:
            value = value + shift_matrix()
        if a > b:
            a, b, value = b, a, value.T
        blocks[a, b] = value

    energies = fin[0, HALF:PART, :] + fin[1, HALF:PART, :]
    mean = jnp.sum(energies, axis=(0, 1), keepdims=True) / TOTAL
    rhs = [jnp.broadcast_to(energies[a : a + 1, :] - mean, (8, B)) for a in range(4)]

    upper = {}
    sol = {}
    for s in range(4):
        if s == 0:
            p = first
        else:
            p = jnp.concatenate(invert([blocks[s, s][8 * q : 8 * q + 8] for q in range(16)]), axis=0)
        for j in range(s + 1, 4):
            upper[s, j] = dot(p, blocks[s, j], ((1,), (0,)))
            for i in range(s + 1, j + 1):
                blocks[i, j] = blocks[i, j] - dot(blocks[s, i], upper[s, j], ((0,), (0,)))
        sol[s] = dot(rhs[s], p, ((1,), (0,)))
        for j in range(s + 1, 4):
            rhs[j] = rhs[j] - dot(sol[s], blocks[s, j], ((1,), (0,)))
        for i in range(s):
            sol[i] = sol[i] - dot(sol[s], upper[i, s], ((1,), (1,)))
            for j in range(s + 1, 4):
                upper[i, j] = upper[i, j] - dot(upper[i, s], upper[s, j], ((1,), (0,)))

    scale = -math.sqrt(PARAMS / TOTAL)
    mine = sol[0]
    for a in range(1, 4):
        mine = jnp.where(samp // 8 == a, sol[a], mine)
    coeff_ref[...] = pltpu.roll(mine, (128 - OWN * (samp % 8)) % 128, 1)[0:1, 0:OWN]
    coeffs = jnp.concatenate([sol[a] for a in range(4)], axis=1)
    high = coeffs.astype(BF16).astype(F32)
    middle = (coeffs - high).astype(BF16).astype(F32)
    low = coeffs - high - middle
    terms = jnp.concatenate([high, middle, low, jnp.zeros((8, TOTAL), F32)], axis=0).astype(BF16)
    for slot in range(2):
        total = lax.dot_general(terms, own[slot], (((1,), (0,)), ((), ())), preferred_element_type=F32)
        rows[slot] = scale * (total[0:8] + (total[8:16] + total[16:24]))


def local(activations, cotangents, energies):
    act = activations.reshape(OWN, LANES, SITES)
    rows, coeffs = whole(act, cotangents, energies.reshape(1, OWN))
    update = rows.reshape(OUT_OWN, -1)
    return update, coeffs.reshape(OWN)


def solution(mesh):
    return jax.shard_map(
        local,
        mesh=mesh,
        in_specs=(P("samp", None, None, None), P("samp", None, "par", None), P("samp")),
        out_specs=(P("par", None), P("samp")),
        check_vma=False,
    )
```

```python
import math

import jax
import jax.numpy as jnp
from jax import lax
from jax.experimental import pallas as pl
from jax.experimental.pallas import tpu as pltpu
from jax.sharding import PartitionSpec as P

C = 64
SIDE = 16
LAYERS = 2
SITES = SIDE * SIDE
OFFSETS = 9

N_Z, N_XH, N_CORE = 8, 2, 2
N_SAMP = N_Z * N_XH * N_CORE
N_XL, N_Y = 2, 8
N_PAR = N_XL * N_Y
N_X = N_XH * N_XL
OWN = 16
TOTAL = N_SAMP * OWN
OUT_OWN = C // N_PAR
LANES = LAYERS * C
ROWS = OFFSETS * OUT_OWN
EXTRA = ROWS - N_SAMP
PARAMS = LAYERS * C * C * OFFSETS
REG_SHIFT = 0.1

HALF = 640
PART = HALF + 8
PLANE = N_Z * N_Y
TILES = PART // 8
FIRST = 24
FLIP = FIRST + PLANE - 1
LOW = FLIP - (TILES - 1)
SPLIT = 8 * FIRST
PIECES = (
    ((0, 0, 0), (0, 0, 1), (0, 1, 0), (0, 2, 0), (0, 2, 1), (0, 3, 0), (0, 3, 1), (1, 2, 0), (1, 2, 1), (1, 3, 0)),
    ((1, 1, 0), (1, 1, 1), (0, 1, 1), (1, 3, 1), (2, 2, 0), (2, 2, 1), (2, 3, 0), (2, 3, 1), (3, 3, 0), (3, 3, 1)),
)

MESH = pl.DeviceIdType.MESH
F32 = jnp.float32
BF16 = jnp.bfloat16


def remote(src, dst, send, recv, samp, par):
    return pltpu.make_async_remote_copy(
        src_ref=src,
        dst_ref=dst,
        send_sem=send,
        recv_sem=recv,
        device_id=(samp, par),
        device_id_type=MESH,
    )


def far_first(i):
    return (4 + ((i + 1) // 2) * (1 - 2 * (i % 2))) % 8


def whole_kernel(
    act_hbm, cot_hbm, en_hbm, out_ref, coeff_ref,
    act_ref, cot_ref, en_ref, spot, fields, shifted, grads, land, own, chip, part, from_plane, from_x, fin,
    rows, row_land,
    act_sem, cot_sem, en_sem, a2a_send, a2a_recv, ex_send, ex_recv, core_send, core_recv, cx_send, cx_recv, r_send, r_recv, rx_send,
    p_send, p_recv, x_send, x_recv, g_send, g_recv, s_send, s_recv, rx_recv, ready,
):
    samp = lax.axis_index("samp")
    par = lax.axis_index("par")
    z = samp // 4
    x_hi = (samp // 2) % 2
    core = samp % 2
    x_lo = par // N_Y
    y = par % N_Y
    x = x_hi * 2 + x_lo
    sibling = samp + 1 - 2 * core

    act_copy = pltpu.make_async_copy(act_hbm, act_ref, act_sem)
    act_copy.start()
    cot_copy = pltpu.make_async_copy(cot_hbm, cot_ref, cot_sem)
    cot_copy.start()
    en_copy = pltpu.make_async_copy(en_hbm, en_ref, en_sem)
    en_copy.start()

    def samp_peer(i):
        to_z = (z + far_first(i // 4)) % N_Z
        to_x = (x_hi + 1 - (i // 2) % 2) % 2
        return to_z * 4 + to_x * 2 + (core + 1 - i % 2) % 2

    def plane_peer(i):
        to_z = (z + far_first(i // 8)) % N_Z
        to_y = (y + far_first(i % 8)) % N_Y
        return to_z, to_y, to_z * 4 + samp % 4, x_lo * N_Y + to_y

    def x_peer(i):
        to = (x + 3 - i) % N_X
        return z * 4 + (to // 2) * 2 + core, (to % 2) * N_Y + y

    barrier = pltpu.get_barrier_semaphore()

    def greet(to_samp, to_par):
        pl.semaphore_signal(barrier, inc=1, device_id=(to_samp, to_par), device_id_type=MESH)

    def greet_samp(i, _):
        greet(samp_peer(i), par)
        return 0

    def y_peer(i):
        return x_lo * N_Y + (y + far_first(i)) % N_Y

    def greet_y(i, _):
        greet(samp, y_peer(i))
        return 0

    lax.fori_loop(0, N_SAMP - 1, greet_samp, 0)
    lax.fori_loop(0, N_Y - 1, greet_y, 0)
    greet(*x_peer(0))
    greet(*x_peer(2))

    cot_copy.wait()
    fields[:, 0:4, :] = cot_ref[:, 0].astype(F32)
    fields[:, 4:8, :] = cot_ref[:, 1].astype(F32)
    field = fields[...].reshape(OWN * 8, SITES)
    column = lax.broadcasted_iota(jnp.int32, field.shape, 1) % SIDE
    for b in (-1, 0, 1):
        if b == 1:
            moved = jnp.where(column == 0, pltpu.roll(field, SITES - 15, 1), pltpu.roll(field, 1, 1))
        elif b == -1:
            moved = jnp.where(column == 15, pltpu.roll(field, 15, 1), pltpu.roll(field, SITES - 1, 1))
        else:
            moved = field
        for a in (-1, 0, 1):
            k = 3 * (a + 1) + (b + 1)
            turned = moved if a == 0 else pltpu.roll(moved, (16 * a) % SITES, 1)
            shifted[:, 8 * k : 8 * k + 8, :] = turned.reshape(OWN, 8, SITES)

    act_copy.wait()
    en_copy.wait()
    first_layer = lax.broadcasted_iota(jnp.int32, (8, LANES), 1) < C

    half = OWN // 2

    def one_sample(part_no, i):
        s = part_no * half + i
        product = lax.dot_general(
            shifted[s].astype(BF16), act_ref[s], (((1,), (1,)), ((), ())), preferred_element_type=F32
        )
        for k in range(OFFSETS):
            tile = product[8 * k : 8 * k + 8, :]
            mixed = jnp.where(first_layer, tile, pltpu.roll(tile, 4, 0))
            grads[part_no, pl.ds(4 * k * half + i, 4, stride=half), :] = mixed[:4]

    def some_samples(part_no):
        def body(step, _):
            for i in range(4):
                one_sample(part_no, step * 4 + i)
            return 0

        lax.fori_loop(0, half // 4, body, 0)

    here = pl.multiple_of(samp * OWN, OWN)

    def send_groups(part_no):
        there = pl.ds(pl.multiple_of(here + part_no * half, half), half)

        def group(r):
            return grads.at[part_no, pl.ds(pl.multiple_of(r * half, half), half)]

        def send_extra(j, _):
            @pl.when(samp != 8 * j)
            def _():
                remote(group(N_SAMP + j), land.at[1, there], ex_send, ex_recv, 8 * j, par).start()

            return 0

        lax.fori_loop(0, EXTRA, send_extra, 0)

        def send_group(i, _):
            to = samp_peer(i)
            remote(group(to), land.at[0, there], a2a_send, a2a_recv, to, par).start()
            return 0

        lax.fori_loop(0, N_SAMP - 1, send_group, 0)

    some_samples(0)
    pl.semaphore_wait(barrier, N_SAMP - 1 + N_Y - 1 + 2)

    def tell_y(i, _):
        pl.semaphore_signal(ready, inc=1, device_id=(samp, y_peer(i)), device_id_type=MESH)
        return 0

    lax.fori_loop(0, N_Y - 1, tell_y, 0)

    send_groups(0)
    some_samples(1)
    send_groups(1)

    def keep(slot, r):
        for part_no in range(2):
            there = pl.ds(pl.multiple_of(here + part_no * half, half), half)
            land[slot, there, :] = grads[part_no, pl.ds(pl.multiple_of(r * half, half), half), :]

    keep(0, samp)
    is_extra = samp % 8 == 0
    chip_extra = (samp // 2) % 4 == 0

    @pl.when(is_extra)
    def _():
        keep(1, N_SAMP + samp // 8)

    @pl.when(jnp.logical_not(is_extra))
    def _():
        own[1] = jnp.zeros((TOTAL, LANES), BF16)

    @pl.when(jnp.logical_not(chip_extra))
    def _():
        chip[2] = jnp.zeros((TOTAL, LANES), BF16)

    row = lax.broadcasted_iota(jnp.int32, (8, LANES), 0)
    lane = lax.broadcasted_iota(jnp.int32, (8, LANES), 1)
    own_place = (row == samp // 8) & (lane // OWN == samp % 8) & (par == 0)
    spot[...] = jnp.zeros((8, LANES), F32)
    spot[0:1, 0:OWN] = en_ref[...]
    moved = pltpu.roll(spot[...], OWN * (samp % 8), 1)
    part[HALF:PART, :] = jnp.where(own_place, jnp.broadcast_to(moved[0:1, :], (8, LANES)), 0.0)

    def wait_recv(ref, sem):
        remote(ref, ref, a2a_send, sem, samp, par).wait_recv()

    def wait_send(ref, sem):
        remote(ref, ref, sem, a2a_recv, samp, par).wait_send()

    most = (N_SAMP - 1) * OWN

    def centre(slot):
        block = land[slot]
        mean = jnp.sum(block, axis=0, keepdims=True) / TOTAL
        return ((block - mean) * (1.0 / math.sqrt(PARAMS))).astype(BF16)

    @pl.when(is_extra)
    def _():
        wait_recv(land.at[1, pl.ds(0, most)], ex_recv)
        c = centre(1)
        own[1] = c
        chip[2] = c
        remote(chip.at[2], chip.at[2], cx_send, cx_recv, sibling, par).start()

    wait_recv(land.at[0, pl.ds(0, most)], a2a_recv)
    c0 = centre(0)
    own[0] = c0
    chip[core] = c0
    remote(chip.at[core], chip.at[core], core_send, core_recv, sibling, par).start()

    @pl.when(chip_extra & (core == 1))
    def _():
        wait_recv(chip.at[2], cx_recv)

    wait_recv(chip.at[1 - core], core_recv)

    def gram_piece(i):
        (a0, b0, h0), (a1, b1, h1) = PIECES[0][i], PIECES[1][i]
        left0, left1 = 128 * a0 + 64 * h0, 128 * a1 + 64 * h1
        left_row = pl.multiple_of(left0 + core * (left1 - left0), 64)
        right_row = pl.multiple_of(128 * (b0 + core * (b1 - b0)), 128)
        total = jnp.zeros((64, 128), F32)
        for q in range(3):
            left = chip[q, pl.ds(left_row, 64), :]
            right = chip[q, pl.ds(right_row, 128), :]
            total += lax.dot_general(left, right, (((1,), (1,)), ((), ())), preferred_element_type=F32)
        part[64 * i : 64 * i + 64, :] = total

    pl.semaphore_wait(ready, N_Y - 1)

    def place(at_z, at_y):
        return ((at_z * N_Y + at_y) * 13) % PLANE

    me = place(z, y)

    def tile(t):
        return pl.ds(pl.multiple_of(8 * t, 8), 8)

    def reduces(batch, q):
        return q < FIRST if batch == 0 else q >= LOW

    def tile_of(batch, q):
        return jnp.minimum(q, FIRST - 1) if batch == 0 else FLIP - jnp.maximum(q, LOW)

    def send_part(batch):
        def body(i, _):
            to_z, to_y, to_samp, to_par = plane_peer(i)
            q = place(to_z, to_y)

            @pl.when(reduces(batch, q))
            def _():
                remote(
                    part.at[tile(tile_of(batch, q))], from_plane.at[batch, me],
                    p_send.at[batch], p_recv.at[batch], to_samp, to_par,
                ).start()

            return 0

        lax.fori_loop(0, PLANE - 1, body, 0)

    def reduce_plane(batch):
        @pl.when(reduces(batch, me))
        def _():
            from_plane[batch, me] = part[tile(tile_of(batch, me)), :]
            wait_recv(from_plane.at[batch, pl.ds(0, PLANE - 1)], p_recv.at[batch])
            from_x[batch, x] = jnp.sum(from_plane[batch], axis=0)

            def send_x(i, _):
                to_samp, to_par = x_peer(i)
                mine = from_x.at[batch, x]
                remote(mine, mine, x_send.at[batch], x_recv.at[batch], to_samp, to_par).start()
                return 0

            lax.fori_loop(0, N_X - 1, send_x, 0)

    def spread_sum(batch):
        @pl.when(reduces(batch, me))
        def _():
            wait_recv(from_x.at[batch, pl.ds(0, N_X - 1)], x_recv.at[batch])
            mine = fin.at[core, tile(tile_of(batch, me))]
            fin[core, tile(tile_of(batch, me)), :] = jnp.sum(from_x[batch], axis=0)

            def send_sum(i, _):
                _, _, to_samp, to_par = plane_peer(i)
                remote(mine, mine, g_send.at[batch], g_recv.at[batch], to_samp, to_par).start()
                return 0

            lax.fori_loop(0, PLANE - 1, send_sum, 0)

    spans = ((0, SPLIT), (SPLIT, PART - SPLIT))

    def span(batch):
        start, size = spans[batch]
        return pl.ds(start, size)

    def gathered(batch):
        start, size = spans[batch]

        @pl.when(reduces(batch, me))
        def _():
            wait_recv(fin.at[core, pl.ds(start, size - 8)], g_recv.at[batch])

        @pl.when(jnp.logical_not(reduces(batch, me)))
        def _():
            wait_recv(fin.at[core, pl.ds(start, size)], g_recv.at[batch])

        remote(
            fin.at[core, span(batch)], fin.at[core, span(batch)], s_send.at[batch], s_recv.at[batch], sibling, par
        ).start()

    def complete(batch):
        wait_recv(fin.at[1 - core, span(batch)], s_recv.at[batch])

    for i in range(3):
        gram_piece(i)
    send_part(0)
    for i in range(3, 10):
        gram_piece(i)
    send_part(1)
    reduce_plane(0)
    reduce_plane(1)
    spread_sum(0)
    spread_sum(1)
    gathered(0)
    complete(0)
    first = join(invert(split(gram_block(fin, 0, 0))))
    across = gram_block(fin, 0, 1)
    above = dot(first, across, ((1,), (0,)))
    second = invert(split(gram_block(fin, 1, 1) - dot(across, above, ((0,), (0,)))), range(4))
    gathered(1)
    second = join(invert(second, range(4, 8)))
    complete(1)

    solve(first, above, second, fin, own, coeff_ref, rows, samp)

    extra = N_SAMP + samp // 8

    @pl.when(is_extra)
    def _():
        def send_second(i, _):
            remote(rows.at[1, pl.ds(0, 1)], row_land.at[extra, pl.ds(0, 1)], rx_send, rx_recv.at[samp // 8], samp_peer(i), par).start()
            return 0

        lax.fori_loop(0, N_SAMP - 1, send_second, 0)
        row_land[extra] = rows[1]

    def send_row(i, _):
        remote(rows.at[0, pl.ds(0, 1)], row_land.at[samp, pl.ds(0, 1)], r_send, r_recv, samp_peer(i), par).start()
        return 0

    lax.fori_loop(0, N_SAMP - 1, send_row, 0)
    row_land[samp] = rows[0]

    wait_send(land.at[0, pl.ds(0, most)], a2a_send)

    def sent_extra(j, _):
        @pl.when(samp != 8 * j)
        def _():
            wait_send(land.at[1, pl.ds(0, OWN)], ex_send)

        return 0

    lax.fori_loop(0, EXTRA, sent_extra, 0)
    wait_send(chip.at[core], core_send)

    @pl.when(is_extra)
    def _():
        wait_send(chip.at[2], cx_send)

    for batch in range(2):

        @pl.when(reduces(batch, me))
        def _():
            wait_send(part.at[pl.ds(0, spans[batch][1] - 8)], p_send.at[batch])
            wait_send(from_x.at[batch, pl.ds(0, N_X - 1)], x_send.at[batch])
            wait_send(from_plane.at[batch, pl.ds(0, PLANE - 1)], g_send.at[batch])

        @pl.when(jnp.logical_not(reduces(batch, me)))
        def _():
            wait_send(part.at[pl.ds(0, spans[batch][1])], p_send.at[batch])

        wait_send(fin.at[core, span(batch)], s_send.at[batch])

    others = row_land.at[pl.ds(0, N_SAMP - 1), pl.ds(0, 1)]
    wait_recv(others, r_recv)

    def await_extra(j, _):
        @pl.when(samp != 8 * j)
        def _():
            wait_recv(row_land.at[0, pl.ds(0, 1)], rx_recv.at[j])

        return 0

    lax.fori_loop(0, EXTRA, await_extra, 0)
    for k in range(OFFSETS):
        for o in range(OUT_OWN):
            out_ref[o, k : k + 1, :] = row_land[k * OUT_OWN + o, 0:1, :]
    wait_send(others, r_send)

    @pl.when(is_extra)
    def _():
        wait_send(others, rx_send)


def whole(act, cot, energies):
    dma = pltpu.SemaphoreType.DMA
    vmem = pl.BlockSpec(memory_space=pltpu.VMEM)
    hbm = pl.BlockSpec(memory_space=pltpu.HBM)
    return pl.pallas_call(
        whole_kernel,
        out_shape=(
            jax.ShapeDtypeStruct((OUT_OWN, OFFSETS, LANES), F32),
            jax.ShapeDtypeStruct((1, OWN), F32),
        ),
        in_specs=[hbm, hbm, hbm],
        out_specs=(vmem, vmem),
        scratch_shapes=[
            pltpu.VMEM((OWN, LANES, SITES), BF16),
            pltpu.VMEM((OWN, LAYERS, OUT_OWN, SITES), BF16),
            pltpu.VMEM((1, OWN), F32),
            pltpu.VMEM((8, LANES), F32),
            pltpu.VMEM((OWN, 8, SITES), F32),
            pltpu.VMEM((OWN, 8 * OFFSETS, SITES), F32),
            pltpu.VMEM((2, ROWS * OWN // 2, LANES), F32),
            pltpu.VMEM((2, TOTAL, LANES), F32),
            pltpu.VMEM((2, TOTAL, LANES), BF16),
            pltpu.VMEM((3, TOTAL, LANES), BF16),
            pltpu.VMEM((PART, LANES), F32),
            pltpu.VMEM((2, PLANE, 8, LANES), F32),
            pltpu.VMEM((2, N_X, 8, LANES), F32),
            pltpu.VMEM((N_CORE, PART, LANES), F32),
            pltpu.VMEM((2, 8, 128), F32),
            pltpu.VMEM((ROWS, 8, LANES), F32),
        ]
        + [dma] * 14
        + [dma((2,))] * 8
        + [dma((EXTRA,)), pltpu.SemaphoreType.REGULAR],
        compiler_params=pltpu.CompilerParams(
            collective_id=0, has_side_effects=True, vmem_limit_bytes=60 * 2**20
        ),
    )(act, cot, energies)


def dot(left, right, dims):
    return lax.dot_general(
        left, right, (dims, ((), ())), precision=lax.Precision.HIGHEST, preferred_element_type=F32
    )


def tree_sum(terms):
    while len(terms) > 1:
        paired = [terms[i] + terms[i + 1] for i in range(0, len(terms) - 1, 2)]
        terms = paired + terms[2 * len(paired) :]
    return terms[0]


def gram_block(fin, a, b):
    halves = []
    for h in range(2):
        core = 0 if (a, b, h) in PIECES[0] else 1
        i = PIECES[core].index((a, b, h))
        halves.append(fin[core, 64 * i : 64 * i + 64, :])
    value = jnp.concatenate(halves, axis=0)
    return value + shift_matrix() if a == b else value


def split(matrix):
    return [matrix[8 * q : 8 * q + 8] for q in range(16)]


def join(tiles):
    return jnp.concatenate(tiles, axis=0)


def invert(tiles, panels=range(8)):
    tiles = list(tiles)
    lane = lax.broadcasted_iota(jnp.int32, (8, 128), 1)
    sub = lax.broadcasted_iota(jnp.int32, (8, 128), 0)
    on = [sub == r for r in range(8)]
    zero = jnp.zeros((8, 128), F32)

    def along_lanes(v, j):
        return jnp.broadcast_to(v[:, j : j + 1], (8, 128))

    def along_rows(v, j):
        return jnp.broadcast_to(v[j : j + 1, :], (8, 128))

    for p in panels:
        base = 16 * p
        inside = (lane >= base) & (lane < base + 16)
        pivot_rows = tiles[2 * p : 2 * p + 2]
        cols = [[along_lanes(v, base + m) for m in range(16)] for v in pivot_rows]
        work = [
            jnp.where(inside, jnp.where(lane - base - 8 * t == sub, 1.0, 0.0), v) for t, v in enumerate(pivot_rows)
        ]
        for j in range(16):
            h, r = divmod(j, 8)
            inverse = 1.0 / along_rows(cols[h][j], r)

            def sweep(pair):
                turned = along_rows(pair[h], r) * inverse
                new = [pair[t] - cols[t][j] * turned for t in range(2)]
                new[h] = jnp.where(on[r], turned, new[h])
                return new

            for m in range(j + 1, 16):
                cols[0][m], cols[1][m] = sweep((cols[0][m], cols[1][m]))
            work = sweep(work)
        spread = [along_rows(work[j // 8], j % 8) for j in range(16)]
        near = [2 * p + 2, 2 * p + 3] if p < 7 else []
        rest = [q for q in range(16) if q not in near and q // 2 != p]
        new = {}
        for q in near:
            new[q] = jnp.where(inside, 0.0, tiles[q]) - tree_sum(
                [along_lanes(tiles[q], base + j) * spread[j] for j in range(16)]
            )
        left = jnp.concatenate([tiles[q] for q in rest], axis=0)
        right = jnp.concatenate([work[q - 2 * p] if q // 2 == p else zero for q in range(16)], axis=0)
        product = dot(left, right, ((1,), (0,)))
        for i, q in enumerate(rest):
            new[q] = jnp.where(inside, 0.0, tiles[q]) - product[8 * i : 8 * i + 8]
        for q in new:
            tiles[q] = new[q]
        tiles[2 * p : 2 * p + 2] = work
    return tiles


def shift_matrix():
    return jnp.where(
        lax.broadcasted_iota(jnp.int32, (128, 128), 0) == lax.broadcasted_iota(jnp.int32, (128, 128), 1),
        REG_SHIFT, 0.0,
    ).astype(F32)


def solve(first, above, second, fin, own, coeff_ref, rows, samp):
    B = 128
    blocks = {(a, b): gram_block(fin, a, b) for a in range(4) for b in range(a, 4)}

    energies = fin[0, HALF:PART, :] + fin[1, HALF:PART, :]
    mean = jnp.sum(energies, axis=(0, 1), keepdims=True) / TOTAL
    rhs = [jnp.broadcast_to(energies[a : a + 1, :] - mean, (8, B)) for a in range(4)]

    upper = {}
    sol = {}
    for s in range(4):
        p = (first, second)[s] if s < 2 else join(invert(split(blocks[s, s])))
        for j in range(s + 1, 4):
            upper[s, j] = above if (s, j) == (0, 1) else dot(p, blocks[s, j], ((1,), (0,)))
            for i in range(s + 1, j + 1):
                if (s, i, j) == (0, 1, 1):
                    continue
                blocks[i, j] = blocks[i, j] - dot(blocks[s, i], upper[s, j], ((0,), (0,)))
        sol[s] = dot(rhs[s], p, ((1,), (0,)))
        for j in range(s + 1, 4):
            rhs[j] = rhs[j] - dot(sol[s], blocks[s, j], ((1,), (0,)))
        for i in range(s):
            sol[i] = sol[i] - dot(sol[s], upper[i, s], ((1,), (1,)))
            for j in range(s + 1, 4):
                upper[i, j] = upper[i, j] - dot(upper[i, s], upper[s, j], ((1,), (0,)))

    scale = -math.sqrt(PARAMS / TOTAL)
    mine = sol[0]
    for a in range(1, 4):
        mine = jnp.where(samp // 8 == a, sol[a], mine)
    coeff_ref[...] = pltpu.roll(mine, (128 - OWN * (samp % 8)) % 128, 1)[0:1, 0:OWN]
    coeffs = jnp.concatenate([sol[a] for a in range(4)], axis=1)
    high = coeffs.astype(BF16).astype(F32)
    middle = (coeffs - high).astype(BF16).astype(F32)
    low = coeffs - high - middle
    terms = jnp.concatenate([high, middle, low, jnp.zeros((8, TOTAL), F32)], axis=0).astype(BF16)
    for slot in range(2):
        total = lax.dot_general(terms, own[slot], (((1,), (0,)), ((), ())), preferred_element_type=F32)
        rows[slot] = scale * (total[0:8] + (total[8:16] + total[16:24]))


def local(activations, cotangents, energies):
    act = activations.reshape(OWN, LANES, SITES)
    rows, coeffs = whole(act, cotangents, energies.reshape(1, OWN))
    update = rows.transpose(0, 2, 1).reshape(OUT_OWN, -1)
    return update, coeffs.reshape(OWN)


def solution(mesh):
    return jax.shard_map(
        local,
        mesh=mesh,
        in_specs=(P("samp", None, None, None), P("samp", None, "par", None), P("samp")),
        out_specs=(P("par", None), P("samp")),
        check_vma=False,
    )
```

```python
import math

import jax
import jax.numpy as jnp
from jax import lax
from jax.experimental import pallas as pl
from jax.experimental.pallas import tpu as pltpu
from jax.sharding import PartitionSpec as P

C = 64
SIDE = 16
LAYERS = 2
SITES = SIDE * SIDE
OFFSETS = 9

N_Z, N_XH, N_CORE = 8, 2, 2
N_SAMP = N_Z * N_XH * N_CORE
N_XL, N_Y = 2, 8
N_PAR = N_XL * N_Y
N_X = N_XH * N_XL
OWN = 16
TOTAL = N_SAMP * OWN
OUT_OWN = C // N_PAR
LANES = LAYERS * C
ROWS = OFFSETS * OUT_OWN
EXTRA = ROWS - N_SAMP
PARAMS = LAYERS * C * C * OFFSETS
REG_SHIFT = 0.1

HALF = 640
PART = HALF + 8
PLANE = N_Z * N_Y
TILES = PART // 8
FIRST = 24
FLIP = FIRST + PLANE - 1
LOW = FLIP - (TILES - 1)
SPLIT = 8 * FIRST
PIECES = (
    ((0, 0, 0), (0, 0, 1), (0, 1, 0), (0, 2, 0), (0, 2, 1), (0, 3, 0), (0, 3, 1), (1, 2, 0), (1, 2, 1), (1, 3, 0)),
    ((1, 1, 0), (1, 1, 1), (0, 1, 1), (1, 3, 1), (2, 2, 0), (2, 2, 1), (2, 3, 0), (2, 3, 1), (3, 3, 0), (3, 3, 1)),
)

MESH = pl.DeviceIdType.MESH
F32 = jnp.float32
BF16 = jnp.bfloat16


def remote(src, dst, send, recv, samp, par):
    return pltpu.make_async_remote_copy(
        src_ref=src,
        dst_ref=dst,
        send_sem=send,
        recv_sem=recv,
        device_id=(samp, par),
        device_id_type=MESH,
    )


def far_first(i):
    return (4 + ((i + 1) // 2) * (1 - 2 * (i % 2))) % 8


def whole_kernel(
    act_hbm, cot_hbm, en_hbm, out_ref, coeff_ref,
    act_ref, cot_ref, en_ref, spot, fields, shifted, grads, land, own, chip, part, from_plane, from_x, fin,
    rows, row_land,
    act_sem, cot_sem, en_sem, a2a_send, a2a_recv, ex_send, ex_recv, core_send, core_recv, cx_send, cx_recv, r_send, r_recv, rx_send,
    p_send, p_recv, x_send, x_recv, g_send, g_recv, s_send, s_recv, rx_recv, ready,
):
    samp = lax.axis_index("samp")
    par = lax.axis_index("par")
    z = samp // 4
    x_hi = (samp // 2) % 2
    core = samp % 2
    x_lo = par // N_Y
    y = par % N_Y
    x = x_hi * 2 + x_lo
    sibling = samp + 1 - 2 * core

    act_copy = pltpu.make_async_copy(act_hbm, act_ref, act_sem)
    act_copy.start()
    cot_copy = pltpu.make_async_copy(cot_hbm, cot_ref, cot_sem)
    cot_copy.start()
    en_copy = pltpu.make_async_copy(en_hbm, en_ref, en_sem)
    en_copy.start()

    def samp_peer(i):
        to_z = (z + far_first(i // 4)) % N_Z
        to_x = (x_hi + 1 - (i // 2) % 2) % 2
        return to_z * 4 + to_x * 2 + (core + 1 - i % 2) % 2

    def plane_peer(i):
        to_z = (z + far_first(i // 8)) % N_Z
        to_y = (y + far_first(i % 8)) % N_Y
        return to_z, to_y, to_z * 4 + samp % 4, x_lo * N_Y + to_y

    def x_peer(i):
        to = (x + 3 - i) % N_X
        return z * 4 + (to // 2) * 2 + core, (to % 2) * N_Y + y

    barrier = pltpu.get_barrier_semaphore()

    def greet(to_samp, to_par):
        pl.semaphore_signal(barrier, inc=1, device_id=(to_samp, to_par), device_id_type=MESH)

    def greet_samp(i, _):
        greet(samp_peer(i), par)
        return 0

    def y_peer(i):
        return x_lo * N_Y + (y + far_first(i)) % N_Y

    def greet_y(i, _):
        greet(samp, y_peer(i))
        return 0

    lax.fori_loop(0, N_SAMP - 1, greet_samp, 0)
    lax.fori_loop(0, N_Y - 1, greet_y, 0)
    greet(*x_peer(0))
    greet(*x_peer(2))

    cot_copy.wait()
    fields[:, 0:4, :] = cot_ref[:, 0].astype(F32)
    fields[:, 4:8, :] = cot_ref[:, 1].astype(F32)
    field = fields[...].reshape(OWN * 8, SITES)
    column = lax.broadcasted_iota(jnp.int32, field.shape, 1) % SIDE
    for b in (-1, 0, 1):
        if b == 1:
            moved = jnp.where(column == 0, pltpu.roll(field, SITES - 15, 1), pltpu.roll(field, 1, 1))
        elif b == -1:
            moved = jnp.where(column == 15, pltpu.roll(field, 15, 1), pltpu.roll(field, SITES - 1, 1))
        else:
            moved = field
        for a in (-1, 0, 1):
            k = 3 * (a + 1) + (b + 1)
            turned = moved if a == 0 else pltpu.roll(moved, (16 * a) % SITES, 1)
            shifted[:, 8 * k : 8 * k + 8, :] = turned.reshape(OWN, 8, SITES)

    act_copy.wait()
    en_copy.wait()
    first_layer = lax.broadcasted_iota(jnp.int32, (8, LANES), 1) < C

    half = OWN // 2

    def one_sample(part_no, i):
        s = part_no * half + i
        product = lax.dot_general(
            shifted[s].astype(BF16), act_ref[s], (((1,), (1,)), ((), ())), preferred_element_type=F32
        )
        for k in range(OFFSETS):
            tile = product[8 * k : 8 * k + 8, :]
            mixed = jnp.where(first_layer, tile, pltpu.roll(tile, 4, 0))
            grads[part_no, pl.ds(4 * k * half + i, 4, stride=half), :] = mixed[:4]

    def some_samples(part_no):
        def body(step, _):
            for i in range(4):
                one_sample(part_no, step * 4 + i)
            return 0

        lax.fori_loop(0, half // 4, body, 0)

    here = pl.multiple_of(samp * OWN, OWN)

    def send_groups(part_no):
        there = pl.ds(pl.multiple_of(here + part_no * half, half), half)

        def group(r):
            return grads.at[part_no, pl.ds(pl.multiple_of(r * half, half), half)]

        def send_extra(j, _):
            @pl.when(samp != 8 * j)
            def _():
                remote(group(N_SAMP + j), land.at[1, there], ex_send, ex_recv, 8 * j, par).start()

            return 0

        lax.fori_loop(0, EXTRA, send_extra, 0)

        def send_group(i, _):
            to = samp_peer(i)
            remote(group(to), land.at[0, there], a2a_send, a2a_recv, to, par).start()
            return 0

        lax.fori_loop(0, N_SAMP - 1, send_group, 0)

    some_samples(0)
    pl.semaphore_wait(barrier, N_SAMP - 1 + N_Y - 1 + 2)

    def tell_y(i, _):
        pl.semaphore_signal(ready, inc=1, device_id=(samp, y_peer(i)), device_id_type=MESH)
        return 0

    lax.fori_loop(0, N_Y - 1, tell_y, 0)

    send_groups(0)
    some_samples(1)
    send_groups(1)

    def keep(slot, r):
        for part_no in range(2):
            there = pl.ds(pl.multiple_of(here + part_no * half, half), half)
            land[slot, there, :] = grads[part_no, pl.ds(pl.multiple_of(r * half, half), half), :]

    keep(0, samp)
    is_extra = samp % 8 == 0
    chip_extra = (samp // 2) % 4 == 0

    @pl.when(is_extra)
    def _():
        keep(1, N_SAMP + samp // 8)

    @pl.when(jnp.logical_not(is_extra))
    def _():
        own[1] = jnp.zeros((TOTAL, LANES), BF16)

    @pl.when(jnp.logical_not(chip_extra))
    def _():
        chip[2] = jnp.zeros((TOTAL, LANES), BF16)

    row = lax.broadcasted_iota(jnp.int32, (8, LANES), 0)
    lane = lax.broadcasted_iota(jnp.int32, (8, LANES), 1)
    own_place = (row == samp // 8) & (lane // OWN == samp % 8) & (par == 0)
    spot[...] = jnp.zeros((8, LANES), F32)
    spot[0:1, 0:OWN] = en_ref[...]
    moved = pltpu.roll(spot[...], OWN * (samp % 8), 1)
    part[HALF:PART, :] = jnp.where(own_place, jnp.broadcast_to(moved[0:1, :], (8, LANES)), 0.0)

    def wait_recv(ref, sem):
        remote(ref, ref, a2a_send, sem, samp, par).wait_recv()

    def wait_send(ref, sem):
        remote(ref, ref, sem, a2a_recv, samp, par).wait_send()

    most = (N_SAMP - 1) * OWN

    def centre(slot):
        block = land[slot]
        mean = jnp.sum(block, axis=0, keepdims=True) / TOTAL
        return ((block - mean) * (1.0 / math.sqrt(PARAMS))).astype(BF16)

    @pl.when(is_extra)
    def _():
        wait_recv(land.at[1, pl.ds(0, most)], ex_recv)
        c = centre(1)
        own[1] = c
        chip[2] = c
        remote(chip.at[2], chip.at[2], cx_send, cx_recv, sibling, par).start()

    wait_recv(land.at[0, pl.ds(0, most)], a2a_recv)
    c0 = centre(0)
    own[0] = c0
    chip[core] = c0
    remote(chip.at[core], chip.at[core], core_send, core_recv, sibling, par).start()

    @pl.when(chip_extra & (core == 1))
    def _():
        wait_recv(chip.at[2], cx_recv)

    wait_recv(chip.at[1 - core], core_recv)

    def gram_piece(i):
        (a0, b0, h0), (a1, b1, h1) = PIECES[0][i], PIECES[1][i]
        left0, left1 = 128 * a0 + 64 * h0, 128 * a1 + 64 * h1
        left_row = pl.multiple_of(left0 + core * (left1 - left0), 64)
        right_row = pl.multiple_of(128 * (b0 + core * (b1 - b0)), 128)
        total = jnp.zeros((64, 128), F32)
        for q in range(3):
            left = chip[q, pl.ds(left_row, 64), :]
            right = chip[q, pl.ds(right_row, 128), :]
            total += lax.dot_general(left, right, (((1,), (1,)), ((), ())), preferred_element_type=F32)
        part[64 * i : 64 * i + 64, :] = total

    pl.semaphore_wait(ready, N_Y - 1)

    def place(at_z, at_y):
        return ((at_z * N_Y + at_y) * 13) % PLANE

    me = place(z, y)

    def tile(t):
        return pl.ds(pl.multiple_of(8 * t, 8), 8)

    def reduces(batch, q):
        return q < FIRST if batch == 0 else q >= LOW

    def tile_of(batch, q):
        return jnp.minimum(q, FIRST - 1) if batch == 0 else FLIP - jnp.maximum(q, LOW)

    def send_part(batch):
        def body(i, _):
            to_z, to_y, to_samp, to_par = plane_peer(i)
            q = place(to_z, to_y)

            @pl.when(reduces(batch, q))
            def _():
                remote(
                    part.at[tile(tile_of(batch, q))], from_plane.at[batch, me],
                    p_send.at[batch], p_recv.at[batch], to_samp, to_par,
                ).start()

            return 0

        lax.fori_loop(0, PLANE - 1, body, 0)

    def reduce_plane(batch):
        @pl.when(reduces(batch, me))
        def _():
            from_plane[batch, me] = part[tile(tile_of(batch, me)), :]
            wait_recv(from_plane.at[batch, pl.ds(0, PLANE - 1)], p_recv.at[batch])
            from_x[batch, x] = jnp.sum(from_plane[batch], axis=0)

            def send_x(i, _):
                to_samp, to_par = x_peer(i)
                mine = from_x.at[batch, x]
                remote(mine, mine, x_send.at[batch], x_recv.at[batch], to_samp, to_par).start()
                return 0

            lax.fori_loop(0, N_X - 1, send_x, 0)

    def spread_sum(batch):
        @pl.when(reduces(batch, me))
        def _():
            wait_recv(from_x.at[batch, pl.ds(0, N_X - 1)], x_recv.at[batch])
            mine = fin.at[core, tile(tile_of(batch, me))]
            fin[core, tile(tile_of(batch, me)), :] = jnp.sum(from_x[batch], axis=0)

            def send_sum(i, _):
                _, _, to_samp, to_par = plane_peer(i)
                remote(mine, mine, g_send.at[batch], g_recv.at[batch], to_samp, to_par).start()
                return 0

            lax.fori_loop(0, PLANE - 1, send_sum, 0)

    spans = ((0, SPLIT), (SPLIT, PART - SPLIT))

    def span(batch):
        start, size = spans[batch]
        return pl.ds(start, size)

    def gathered(batch):
        start, size = spans[batch]

        @pl.when(reduces(batch, me))
        def _():
            wait_recv(fin.at[core, pl.ds(start, size - 8)], g_recv.at[batch])

        @pl.when(jnp.logical_not(reduces(batch, me)))
        def _():
            wait_recv(fin.at[core, pl.ds(start, size)], g_recv.at[batch])

        remote(
            fin.at[core, span(batch)], fin.at[core, span(batch)], s_send.at[batch], s_recv.at[batch], sibling, par
        ).start()

    def complete(batch):
        wait_recv(fin.at[1 - core, span(batch)], s_recv.at[batch])

    for i in range(3):
        gram_piece(i)
    send_part(0)
    for i in range(3, 10):
        gram_piece(i)
    send_part(1)
    reduce_plane(0)
    spread_sum(0)
    reduce_plane(1)
    spread_sum(1)
    gathered(0)
    complete(0)
    first = join(invert(split(gram_block(fin, 0, 0))))
    across = gram_block(fin, 0, 1)
    above = dot(first, across, ((1,), (0,)))
    second = invert(split(gram_block(fin, 1, 1) - dot(across, above, ((0,), (0,)))), range(4))
    gathered(1)
    second = join(invert(second, range(4, 8)))
    complete(1)

    solve(first, above, second, fin, own, coeff_ref, rows, samp)

    extra = N_SAMP + samp // 8

    @pl.when(is_extra)
    def _():
        def send_second(i, _):
            remote(rows.at[1, pl.ds(0, 1)], row_land.at[extra, pl.ds(0, 1)], rx_send, rx_recv.at[samp // 8], samp_peer(i), par).start()
            return 0

        lax.fori_loop(0, N_SAMP - 1, send_second, 0)
        row_land[extra] = rows[1]

    def send_row(i, _):
        remote(rows.at[0, pl.ds(0, 1)], row_land.at[samp, pl.ds(0, 1)], r_send, r_recv, samp_peer(i), par).start()
        return 0

    lax.fori_loop(0, N_SAMP - 1, send_row, 0)
    row_land[samp] = rows[0]

    wait_send(land.at[0, pl.ds(0, most)], a2a_send)

    def sent_extra(j, _):
        @pl.when(samp != 8 * j)
        def _():
            wait_send(land.at[1, pl.ds(0, OWN)], ex_send)

        return 0

    lax.fori_loop(0, EXTRA, sent_extra, 0)
    wait_send(chip.at[core], core_send)

    @pl.when(is_extra)
    def _():
        wait_send(chip.at[2], cx_send)

    for batch in range(2):

        @pl.when(reduces(batch, me))
        def _():
            wait_send(part.at[pl.ds(0, spans[batch][1] - 8)], p_send.at[batch])
            wait_send(from_x.at[batch, pl.ds(0, N_X - 1)], x_send.at[batch])
            wait_send(from_plane.at[batch, pl.ds(0, PLANE - 1)], g_send.at[batch])

        @pl.when(jnp.logical_not(reduces(batch, me)))
        def _():
            wait_send(part.at[pl.ds(0, spans[batch][1])], p_send.at[batch])

        wait_send(fin.at[core, span(batch)], s_send.at[batch])

    others = row_land.at[pl.ds(0, N_SAMP - 1), pl.ds(0, 1)]
    wait_recv(others, r_recv)

    def await_extra(j, _):
        @pl.when(samp != 8 * j)
        def _():
            wait_recv(row_land.at[0, pl.ds(0, 1)], rx_recv.at[j])

        return 0

    lax.fori_loop(0, EXTRA, await_extra, 0)
    for k in range(OFFSETS):
        for o in range(OUT_OWN):
            out_ref[o, k : k + 1, :] = row_land[k * OUT_OWN + o, 0:1, :]
    wait_send(others, r_send)

    @pl.when(is_extra)
    def _():
        wait_send(others, rx_send)


def whole(act, cot, energies):
    dma = pltpu.SemaphoreType.DMA
    vmem = pl.BlockSpec(memory_space=pltpu.VMEM)
    hbm = pl.BlockSpec(memory_space=pltpu.HBM)
    return pl.pallas_call(
        whole_kernel,
        out_shape=(
            jax.ShapeDtypeStruct((OUT_OWN, OFFSETS, LANES), F32),
            jax.ShapeDtypeStruct((1, OWN), F32),
        ),
        in_specs=[hbm, hbm, hbm],
        out_specs=(vmem, vmem),
        scratch_shapes=[
            pltpu.VMEM((OWN, LANES, SITES), BF16),
            pltpu.VMEM((OWN, LAYERS, OUT_OWN, SITES), BF16),
            pltpu.VMEM((1, OWN), F32),
            pltpu.VMEM((8, LANES), F32),
            pltpu.VMEM((OWN, 8, SITES), F32),
            pltpu.VMEM((OWN, 8 * OFFSETS, SITES), F32),
            pltpu.VMEM((2, ROWS * OWN // 2, LANES), F32),
            pltpu.VMEM((2, TOTAL, LANES), F32),
            pltpu.VMEM((2, TOTAL, LANES), BF16),
            pltpu.VMEM((3, TOTAL, LANES), BF16),
            pltpu.VMEM((PART, LANES), F32),
            pltpu.VMEM((2, PLANE, 8, LANES), F32),
            pltpu.VMEM((2, N_X, 8, LANES), F32),
            pltpu.VMEM((N_CORE, PART, LANES), F32),
            pltpu.VMEM((2, 8, 128), F32),
            pltpu.VMEM((ROWS, 8, LANES), F32),
        ]
        + [dma] * 14
        + [dma((2,))] * 8
        + [dma((EXTRA,)), pltpu.SemaphoreType.REGULAR],
        compiler_params=pltpu.CompilerParams(
            collective_id=0, has_side_effects=True, vmem_limit_bytes=60 * 2**20
        ),
    )(act, cot, energies)


def dot(left, right, dims):
    return lax.dot_general(
        left, right, (dims, ((), ())), precision=lax.Precision.HIGHEST, preferred_element_type=F32
    )


def tree_sum(terms):
    while len(terms) > 1:
        paired = [terms[i] + terms[i + 1] for i in range(0, len(terms) - 1, 2)]
        terms = paired + terms[2 * len(paired) :]
    return terms[0]


def gram_block(fin, a, b):
    halves = []
    for h in range(2):
        core = 0 if (a, b, h) in PIECES[0] else 1
        i = PIECES[core].index((a, b, h))
        halves.append(fin[core, 64 * i : 64 * i + 64, :])
    value = jnp.concatenate(halves, axis=0)
    return value + shift_matrix() if a == b else value


def split(matrix):
    return [matrix[8 * q : 8 * q + 8] for q in range(16)]


def join(tiles):
    return jnp.concatenate(tiles, axis=0)


def invert(tiles, panels=range(8)):
    tiles = list(tiles)
    lane = lax.broadcasted_iota(jnp.int32, (8, 128), 1)
    sub = lax.broadcasted_iota(jnp.int32, (8, 128), 0)
    on = [sub == r for r in range(8)]
    zero = jnp.zeros((8, 128), F32)

    def along_lanes(v, j):
        return jnp.broadcast_to(v[:, j : j + 1], (8, 128))

    def along_rows(v, j):
        return jnp.broadcast_to(v[j : j + 1, :], (8, 128))

    for p in panels:
        base = 16 * p
        inside = (lane >= base) & (lane < base + 16)
        pivot_rows = tiles[2 * p : 2 * p + 2]
        cols = [[along_lanes(v, base + m) for m in range(16)] for v in pivot_rows]
        work = [
            jnp.where(inside, jnp.where(lane - base - 8 * t == sub, 1.0, 0.0), v) for t, v in enumerate(pivot_rows)
        ]
        for j in range(16):
            h, r = divmod(j, 8)
            inverse = 1.0 / along_rows(cols[h][j], r)

            def sweep(pair):
                turned = along_rows(pair[h], r) * inverse
                new = [pair[t] - cols[t][j] * turned for t in range(2)]
                new[h] = jnp.where(on[r], turned, new[h])
                return new

            for m in range(j + 1, 16):
                cols[0][m], cols[1][m] = sweep((cols[0][m], cols[1][m]))
            work = sweep(work)
        spread = [along_rows(work[j // 8], j % 8) for j in range(16)]
        near = [2 * p + 2, 2 * p + 3] if p < 7 else []
        rest = [q for q in range(16) if q not in near and q // 2 != p]
        new = {}
        for q in near:
            new[q] = jnp.where(inside, 0.0, tiles[q]) - tree_sum(
                [along_lanes(tiles[q], base + j) * spread[j] for j in range(16)]
            )
        left = jnp.concatenate([tiles[q] for q in rest], axis=0)
        right = jnp.concatenate([work[q - 2 * p] if q // 2 == p else zero for q in range(16)], axis=0)
        product = dot(left, right, ((1,), (0,)))
        for i, q in enumerate(rest):
            new[q] = jnp.where(inside, 0.0, tiles[q]) - product[8 * i : 8 * i + 8]
        for q in new:
            tiles[q] = new[q]
        tiles[2 * p : 2 * p + 2] = work
    return tiles


def shift_matrix():
    return jnp.where(
        lax.broadcasted_iota(jnp.int32, (128, 128), 0) == lax.broadcasted_iota(jnp.int32, (128, 128), 1),
        REG_SHIFT, 0.0,
    ).astype(F32)


def solve(first, above, second, fin, own, coeff_ref, rows, samp):
    B = 128
    blocks = {(a, b): gram_block(fin, a, b) for a in range(4) for b in range(a, 4)}

    energies = fin[0, HALF:PART, :] + fin[1, HALF:PART, :]
    mean = jnp.sum(energies, axis=(0, 1), keepdims=True) / TOTAL
    rhs = [jnp.broadcast_to(energies[a : a + 1, :] - mean, (8, B)) for a in range(4)]

    upper = {}
    sol = {}
    for s in range(4):
        p = (first, second)[s] if s < 2 else join(invert(split(blocks[s, s])))
        for j in range(s + 1, 4):
            upper[s, j] = above if (s, j) == (0, 1) else dot(p, blocks[s, j], ((1,), (0,)))
            for i in range(s + 1, j + 1):
                if (s, i, j) == (0, 1, 1):
                    continue
                blocks[i, j] = blocks[i, j] - dot(blocks[s, i], upper[s, j], ((0,), (0,)))
        sol[s] = dot(rhs[s], p, ((1,), (0,)))
        for j in range(s + 1, 4):
            rhs[j] = rhs[j] - dot(sol[s], blocks[s, j], ((1,), (0,)))
        for i in range(s):
            sol[i] = sol[i] - dot(sol[s], upper[i, s], ((1,), (1,)))
            for j in range(s + 1, 4):
                upper[i, j] = upper[i, j] - dot(upper[i, s], upper[s, j], ((1,), (0,)))

    scale = -math.sqrt(PARAMS / TOTAL)
    mine = sol[0]
    for a in range(1, 4):
        mine = jnp.where(samp // 8 == a, sol[a], mine)
    coeff_ref[...] = pltpu.roll(mine, (128 - OWN * (samp % 8)) % 128, 1)[0:1, 0:OWN]
    coeffs = jnp.concatenate([sol[a] for a in range(4)], axis=1)
    high = coeffs.astype(BF16).astype(F32)
    middle = (coeffs - high).astype(BF16).astype(F32)
    low = coeffs - high - middle
    terms = jnp.concatenate([high, middle, low, jnp.zeros((8, TOTAL), F32)], axis=0).astype(BF16)
    for slot in range(2):
        total = lax.dot_general(terms, own[slot], (((1,), (0,)), ((), ())), preferred_element_type=F32)
        rows[slot] = scale * (total[0:8] + (total[8:16] + total[16:24]))


def local(activations, cotangents, energies):
    act = activations.reshape(OWN, LANES, SITES)
    rows, coeffs = whole(act, cotangents, energies.reshape(1, OWN))
    update = rows.transpose(0, 2, 1).reshape(OUT_OWN, -1)
    return update, coeffs.reshape(OWN)


def solution(mesh):
    return jax.shard_map(
        local,
        mesh=mesh,
        in_specs=(P("samp", None, None, None), P("samp", None, "par", None), P("samp")),
        out_specs=(P("par", None), P("samp")),
        check_vma=False,
    )
```

```python
import math

import jax
import jax.numpy as jnp
from jax import lax
from jax.experimental import pallas as pl
from jax.experimental.pallas import tpu as pltpu
from jax.sharding import PartitionSpec as P

C = 64
SIDE = 16
LAYERS = 2
SITES = SIDE * SIDE
OFFSETS = 9

N_Z, N_XH, N_CORE = 8, 2, 2
N_SAMP = N_Z * N_XH * N_CORE
N_XL, N_Y = 2, 8
N_PAR = N_XL * N_Y
N_X = N_XH * N_XL
OWN = 16
TOTAL = N_SAMP * OWN
OUT_OWN = C // N_PAR
LANES = LAYERS * C
ROWS = OFFSETS * OUT_OWN
EXTRA = ROWS - N_SAMP
PARAMS = LAYERS * C * C * OFFSETS
REG_SHIFT = 0.1

HALF = 640
PART = HALF + 8
PLANE = N_Z * N_Y
TILES = PART // 8
FIRST = 24
FLIP = FIRST + PLANE - 1
LOW = FLIP - (TILES - 1)
SPLIT = 8 * FIRST
PIECES = (
    ((0, 0, 0), (0, 0, 1), (0, 1, 0), (0, 2, 0), (0, 2, 1), (0, 3, 0), (0, 3, 1), (1, 2, 0), (1, 2, 1), (1, 3, 0)),
    ((1, 1, 0), (1, 1, 1), (0, 1, 1), (1, 3, 1), (2, 2, 0), (2, 2, 1), (2, 3, 0), (2, 3, 1), (3, 3, 0), (3, 3, 1)),
)

MESH = pl.DeviceIdType.MESH
F32 = jnp.float32
BF16 = jnp.bfloat16


def remote(src, dst, send, recv, samp, par):
    return pltpu.make_async_remote_copy(
        src_ref=src,
        dst_ref=dst,
        send_sem=send,
        recv_sem=recv,
        device_id=(samp, par),
        device_id_type=MESH,
    )


def far_first(i):
    return (4 + ((i + 1) // 2) * (1 - 2 * (i % 2))) % 8


def whole_kernel(
    act_hbm, cot_hbm, en_hbm, out_ref, coeff_ref,
    act_ref, cot_ref, en_ref, spot, fields, shifted, grads, land, own, chip, part, from_plane, from_x, fin,
    rows, row_land,
    act_sem, cot_sem, en_sem, a2a_send, a2a_recv, ex_send, ex_recv, core_send, core_recv, cx_send, cx_recv, r_send, r_recv, rx_send,
    p_send, p_recv, x_send, x_recv, g_send, g_recv, s_send, s_recv, rx_recv, ready,
):
    samp = lax.axis_index("samp")
    par = lax.axis_index("par")
    z = samp // 4
    x_hi = (samp // 2) % 2
    core = samp % 2
    x_lo = par // N_Y
    y = par % N_Y
    x = x_hi * 2 + x_lo
    sibling = samp + 1 - 2 * core

    act_copy = pltpu.make_async_copy(act_hbm, act_ref, act_sem)
    act_copy.start()
    cot_copy = pltpu.make_async_copy(cot_hbm, cot_ref, cot_sem)
    cot_copy.start()
    en_copy = pltpu.make_async_copy(en_hbm, en_ref, en_sem)
    en_copy.start()

    def samp_peer(i):
        to_z = (z + far_first(i // 4)) % N_Z
        to_x = (x_hi + 1 - (i // 2) % 2) % 2
        return to_z * 4 + to_x * 2 + (core + 1 - i % 2) % 2

    def plane_peer(i):
        to_z = (z + far_first(i // 8)) % N_Z
        to_y = (y + far_first(i % 8)) % N_Y
        return to_z, to_y, to_z * 4 + samp % 4, x_lo * N_Y + to_y

    def x_peer(i):
        to = (x + 3 - i) % N_X
        return z * 4 + (to // 2) * 2 + core, (to % 2) * N_Y + y

    barrier = pltpu.get_barrier_semaphore()

    def greet(to_samp, to_par):
        pl.semaphore_signal(barrier, inc=1, device_id=(to_samp, to_par), device_id_type=MESH)

    def greet_samp(i, _):
        greet(samp_peer(i), par)
        return 0

    def y_peer(i):
        return x_lo * N_Y + (y + far_first(i)) % N_Y

    def greet_y(i, _):
        greet(samp, y_peer(i))
        return 0

    lax.fori_loop(0, N_SAMP - 1, greet_samp, 0)
    lax.fori_loop(0, N_Y - 1, greet_y, 0)
    greet(*x_peer(0))
    greet(*x_peer(2))

    cot_copy.wait()
    fields[:, 0:4, :] = cot_ref[:, 0].astype(F32)
    fields[:, 4:8, :] = cot_ref[:, 1].astype(F32)
    field = fields[...].reshape(OWN * 8, SITES)
    column = lax.broadcasted_iota(jnp.int32, field.shape, 1) % SIDE
    for b in (-1, 0, 1):
        if b == 1:
            moved = jnp.where(column == 0, pltpu.roll(field, SITES - 15, 1), pltpu.roll(field, 1, 1))
        elif b == -1:
            moved = jnp.where(column == 15, pltpu.roll(field, 15, 1), pltpu.roll(field, SITES - 1, 1))
        else:
            moved = field
        for a in (-1, 0, 1):
            k = 3 * (a + 1) + (b + 1)
            turned = moved if a == 0 else pltpu.roll(moved, (16 * a) % SITES, 1)
            shifted[:, 8 * k : 8 * k + 8, :] = turned.reshape(OWN, 8, SITES)

    act_copy.wait()
    en_copy.wait()
    first_layer = lax.broadcasted_iota(jnp.int32, (8, LANES), 1) < C

    half = OWN // 2

    def one_sample(part_no, i):
        s = part_no * half + i
        product = lax.dot_general(
            shifted[s].astype(BF16), act_ref[s], (((1,), (1,)), ((), ())), preferred_element_type=F32
        )
        for k in range(OFFSETS):
            tile = product[8 * k : 8 * k + 8, :]
            mixed = jnp.where(first_layer, tile, pltpu.roll(tile, 4, 0))
            grads[part_no, pl.ds(4 * k * half + i, 4, stride=half), :] = mixed[:4]

    def some_samples(part_no):
        def body(step, _):
            for i in range(4):
                one_sample(part_no, step * 4 + i)
            return 0

        lax.fori_loop(0, half // 4, body, 0)

    here = pl.multiple_of(samp * OWN, OWN)

    def send_groups(part_no):
        there = pl.ds(pl.multiple_of(here + part_no * half, half), half)

        def group(r):
            return grads.at[part_no, pl.ds(pl.multiple_of(r * half, half), half)]

        def send_extra(j, _):
            @pl.when(samp != 8 * j)
            def _():
                remote(group(N_SAMP + j), land.at[1, there], ex_send, ex_recv, 8 * j, par).start()

            return 0

        lax.fori_loop(0, EXTRA, send_extra, 0)

        def send_group(i, _):
            to = samp_peer(i)
            remote(group(to), land.at[0, there], a2a_send, a2a_recv, to, par).start()
            return 0

        lax.fori_loop(0, N_SAMP - 1, send_group, 0)

    some_samples(0)
    pl.semaphore_wait(barrier, N_SAMP - 1 + N_Y - 1 + 2)

    def tell_y(i, _):
        pl.semaphore_signal(ready, inc=1, device_id=(samp, y_peer(i)), device_id_type=MESH)
        return 0

    lax.fori_loop(0, N_Y - 1, tell_y, 0)

    send_groups(0)
    some_samples(1)
    send_groups(1)

    def keep(slot, r):
        for part_no in range(2):
            there = pl.ds(pl.multiple_of(here + part_no * half, half), half)
            land[slot, there, :] = grads[part_no, pl.ds(pl.multiple_of(r * half, half), half), :]

    keep(0, samp)
    is_extra = samp % 8 == 0
    chip_extra = (samp // 2) % 4 == 0

    @pl.when(is_extra)
    def _():
        keep(1, N_SAMP + samp // 8)

    @pl.when(jnp.logical_not(is_extra))
    def _():
        own[1] = jnp.zeros((TOTAL, LANES), BF16)

    @pl.when(jnp.logical_not(chip_extra))
    def _():
        chip[2] = jnp.zeros((TOTAL, LANES), BF16)

    row = lax.broadcasted_iota(jnp.int32, (8, LANES), 0)
    lane = lax.broadcasted_iota(jnp.int32, (8, LANES), 1)
    own_place = (row == samp // 8) & (lane // OWN == samp % 8) & (par == 0)
    spot[...] = jnp.zeros((8, LANES), F32)
    spot[0:1, 0:OWN] = en_ref[...]
    moved = pltpu.roll(spot[...], OWN * (samp % 8), 1)
    part[HALF:PART, :] = jnp.where(own_place, jnp.broadcast_to(moved[0:1, :], (8, LANES)), 0.0)

    def wait_recv(ref, sem):
        remote(ref, ref, a2a_send, sem, samp, par).wait_recv()

    def wait_send(ref, sem):
        remote(ref, ref, sem, a2a_recv, samp, par).wait_send()

    most = (N_SAMP - 1) * OWN

    def centre(slot):
        block = land[slot]
        mean = jnp.sum(block, axis=0, keepdims=True) / TOTAL
        return ((block - mean) * (1.0 / math.sqrt(PARAMS))).astype(BF16)

    @pl.when(is_extra)
    def _():
        wait_recv(land.at[1, pl.ds(0, most)], ex_recv)
        c = centre(1)
        own[1] = c
        chip[2] = c
        remote(chip.at[2], chip.at[2], cx_send, cx_recv, sibling, par).start()

    wait_recv(land.at[0, pl.ds(0, most)], a2a_recv)
    c0 = centre(0)
    own[0] = c0
    chip[core] = c0
    remote(chip.at[core], chip.at[core], core_send, core_recv, sibling, par).start()

    @pl.when(chip_extra & (core == 1))
    def _():
        wait_recv(chip.at[2], cx_recv)

    wait_recv(chip.at[1 - core], core_recv)

    def gram_piece(i):
        (a0, b0, h0), (a1, b1, h1) = PIECES[0][i], PIECES[1][i]
        left0, left1 = 128 * a0 + 64 * h0, 128 * a1 + 64 * h1
        left_row = pl.multiple_of(left0 + core * (left1 - left0), 64)
        right_row = pl.multiple_of(128 * (b0 + core * (b1 - b0)), 128)
        total = jnp.zeros((64, 128), F32)
        for q in range(3):
            left = chip[q, pl.ds(left_row, 64), :]
            right = chip[q, pl.ds(right_row, 128), :]
            total += lax.dot_general(left, right, (((1,), (1,)), ((), ())), preferred_element_type=F32)
        part[64 * i : 64 * i + 64, :] = total

    pl.semaphore_wait(ready, N_Y - 1)

    def place(at_z, at_y):
        return ((at_z * N_Y + at_y) * 13 + core * (PLANE // 2)) % PLANE

    me = place(z, y)

    def tile(t):
        return pl.ds(pl.multiple_of(8 * t, 8), 8)

    def reduces(batch, q):
        return q < FIRST if batch == 0 else q >= LOW

    def tile_of(batch, q):
        return jnp.minimum(q, FIRST - 1) if batch == 0 else FLIP - jnp.maximum(q, LOW)

    def send_part(batch):
        def body(i, _):
            to_z, to_y, to_samp, to_par = plane_peer(i)
            q = place(to_z, to_y)

            @pl.when(reduces(batch, q))
            def _():
                remote(
                    part.at[tile(tile_of(batch, q))], from_plane.at[batch, me],
                    p_send.at[batch], p_recv.at[batch], to_samp, to_par,
                ).start()

            return 0

        lax.fori_loop(0, PLANE - 1, body, 0)

    def reduce_plane(batch):
        @pl.when(reduces(batch, me))
        def _():
            from_plane[batch, me] = part[tile(tile_of(batch, me)), :]
            wait_recv(from_plane.at[batch, pl.ds(0, PLANE - 1)], p_recv.at[batch])
            from_x[batch, x] = jnp.sum(from_plane[batch], axis=0)

            def send_x(i, _):
                to_samp, to_par = x_peer(i)
                mine = from_x.at[batch, x]
                remote(mine, mine, x_send.at[batch], x_recv.at[batch], to_samp, to_par).start()
                return 0

            lax.fori_loop(0, N_X - 1, send_x, 0)

    def spread_sum(batch):
        @pl.when(reduces(batch, me))
        def _():
            wait_recv(from_x.at[batch, pl.ds(0, N_X - 1)], x_recv.at[batch])
            mine = fin.at[core, tile(tile_of(batch, me))]
            fin[core, tile(tile_of(batch, me)), :] = jnp.sum(from_x[batch], axis=0)

            def send_sum(i, _):
                _, _, to_samp, to_par = plane_peer(i)
                remote(mine, mine, g_send.at[batch], g_recv.at[batch], to_samp, to_par).start()
                return 0

            lax.fori_loop(0, PLANE - 1, send_sum, 0)

    spans = ((0, SPLIT), (SPLIT, PART - SPLIT))

    def span(batch):
        start, size = spans[batch]
        return pl.ds(start, size)

    def gathered(batch):
        start, size = spans[batch]

        @pl.when(reduces(batch, me))
        def _():
            wait_recv(fin.at[core, pl.ds(start, size - 8)], g_recv.at[batch])

        @pl.when(jnp.logical_not(reduces(batch, me)))
        def _():
            wait_recv(fin.at[core, pl.ds(start, size)], g_recv.at[batch])

        remote(
            fin.at[core, span(batch)], fin.at[core, span(batch)], s_send.at[batch], s_recv.at[batch], sibling, par
        ).start()

    def complete(batch):
        wait_recv(fin.at[1 - core, span(batch)], s_recv.at[batch])

    for i in range(3):
        gram_piece(i)
    send_part(0)
    for i in range(3, 10):
        gram_piece(i)
    send_part(1)
    reduce_plane(0)
    spread_sum(0)
    reduce_plane(1)
    spread_sum(1)
    gathered(0)
    complete(0)
    first = join(invert(split(gram_block(fin, 0, 0))))
    across = gram_block(fin, 0, 1)
    above = dot(first, across, ((1,), (0,)))
    second = invert(split(gram_block(fin, 1, 1) - dot(across, above, ((0,), (0,)))), range(4))
    gathered(1)
    second = join(invert(second, range(4, 8)))
    complete(1)

    solve(first, above, second, fin, own, coeff_ref, rows, samp)

    extra = N_SAMP + samp // 8

    @pl.when(is_extra)
    def _():
        def send_second(i, _):
            remote(rows.at[1, pl.ds(0, 1)], row_land.at[extra, pl.ds(0, 1)], rx_send, rx_recv.at[samp // 8], samp_peer(i), par).start()
            return 0

        lax.fori_loop(0, N_SAMP - 1, send_second, 0)
        row_land[extra] = rows[1]

    def send_row(i, _):
        remote(rows.at[0, pl.ds(0, 1)], row_land.at[samp, pl.ds(0, 1)], r_send, r_recv, samp_peer(i), par).start()
        return 0

    lax.fori_loop(0, N_SAMP - 1, send_row, 0)
    row_land[samp] = rows[0]

    wait_send(land.at[0, pl.ds(0, most)], a2a_send)

    def sent_extra(j, _):
        @pl.when(samp != 8 * j)
        def _():
            wait_send(land.at[1, pl.ds(0, OWN)], ex_send)

        return 0

    lax.fori_loop(0, EXTRA, sent_extra, 0)
    wait_send(chip.at[core], core_send)

    @pl.when(is_extra)
    def _():
        wait_send(chip.at[2], cx_send)

    for batch in range(2):

        @pl.when(reduces(batch, me))
        def _():
            wait_send(part.at[pl.ds(0, spans[batch][1] - 8)], p_send.at[batch])
            wait_send(from_x.at[batch, pl.ds(0, N_X - 1)], x_send.at[batch])
            wait_send(from_plane.at[batch, pl.ds(0, PLANE - 1)], g_send.at[batch])

        @pl.when(jnp.logical_not(reduces(batch, me)))
        def _():
            wait_send(part.at[pl.ds(0, spans[batch][1])], p_send.at[batch])

        wait_send(fin.at[core, span(batch)], s_send.at[batch])

    others = row_land.at[pl.ds(0, N_SAMP - 1), pl.ds(0, 1)]
    wait_recv(others, r_recv)

    def await_extra(j, _):
        @pl.when(samp != 8 * j)
        def _():
            wait_recv(row_land.at[0, pl.ds(0, 1)], rx_recv.at[j])

        return 0

    lax.fori_loop(0, EXTRA, await_extra, 0)
    for k in range(OFFSETS):
        for o in range(OUT_OWN):
            out_ref[o, k : k + 1, :] = row_land[k * OUT_OWN + o, 0:1, :]
    wait_send(others, r_send)

    @pl.when(is_extra)
    def _():
        wait_send(others, rx_send)


def whole(act, cot, energies):
    dma = pltpu.SemaphoreType.DMA
    vmem = pl.BlockSpec(memory_space=pltpu.VMEM)
    hbm = pl.BlockSpec(memory_space=pltpu.HBM)
    return pl.pallas_call(
        whole_kernel,
        out_shape=(
            jax.ShapeDtypeStruct((OUT_OWN, OFFSETS, LANES), F32),
            jax.ShapeDtypeStruct((1, OWN), F32),
        ),
        in_specs=[hbm, hbm, hbm],
        out_specs=(vmem, vmem),
        scratch_shapes=[
            pltpu.VMEM((OWN, LANES, SITES), BF16),
            pltpu.VMEM((OWN, LAYERS, OUT_OWN, SITES), BF16),
            pltpu.VMEM((1, OWN), F32),
            pltpu.VMEM((8, LANES), F32),
            pltpu.VMEM((OWN, 8, SITES), F32),
            pltpu.VMEM((OWN, 8 * OFFSETS, SITES), F32),
            pltpu.VMEM((2, ROWS * OWN // 2, LANES), F32),
            pltpu.VMEM((2, TOTAL, LANES), F32),
            pltpu.VMEM((2, TOTAL, LANES), BF16),
            pltpu.VMEM((3, TOTAL, LANES), BF16),
            pltpu.VMEM((PART, LANES), F32),
            pltpu.VMEM((2, PLANE, 8, LANES), F32),
            pltpu.VMEM((2, N_X, 8, LANES), F32),
            pltpu.VMEM((N_CORE, PART, LANES), F32),
            pltpu.VMEM((2, 8, 128), F32),
            pltpu.VMEM((ROWS, 8, LANES), F32),
        ]
        + [dma] * 14
        + [dma((2,))] * 8
        + [dma((EXTRA,)), pltpu.SemaphoreType.REGULAR],
        compiler_params=pltpu.CompilerParams(
            collective_id=0, has_side_effects=True, vmem_limit_bytes=60 * 2**20
        ),
    )(act, cot, energies)


def dot(left, right, dims):
    return lax.dot_general(
        left, right, (dims, ((), ())), precision=lax.Precision.HIGHEST, preferred_element_type=F32
    )


def tree_sum(terms):
    while len(terms) > 1:
        paired = [terms[i] + terms[i + 1] for i in range(0, len(terms) - 1, 2)]
        terms = paired + terms[2 * len(paired) :]
    return terms[0]


def gram_block(fin, a, b):
    halves = []
    for h in range(2):
        core = 0 if (a, b, h) in PIECES[0] else 1
        i = PIECES[core].index((a, b, h))
        halves.append(fin[core, 64 * i : 64 * i + 64, :])
    value = jnp.concatenate(halves, axis=0)
    return value + shift_matrix() if a == b else value


def split(matrix):
    return [matrix[8 * q : 8 * q + 8] for q in range(16)]


def join(tiles):
    return jnp.concatenate(tiles, axis=0)


def invert(tiles, panels=range(8)):
    tiles = list(tiles)
    lane = lax.broadcasted_iota(jnp.int32, (8, 128), 1)
    sub = lax.broadcasted_iota(jnp.int32, (8, 128), 0)
    on = [sub == r for r in range(8)]
    zero = jnp.zeros((8, 128), F32)

    def along_lanes(v, j):
        return jnp.broadcast_to(v[:, j : j + 1], (8, 128))

    def along_rows(v, j):
        return jnp.broadcast_to(v[j : j + 1, :], (8, 128))

    for p in panels:
        base = 16 * p
        inside = (lane >= base) & (lane < base + 16)
        pivot_rows = tiles[2 * p : 2 * p + 2]
        cols = [[along_lanes(v, base + m) for m in range(16)] for v in pivot_rows]
        work = [
            jnp.where(inside, jnp.where(lane - base - 8 * t == sub, 1.0, 0.0), v) for t, v in enumerate(pivot_rows)
        ]
        for j in range(16):
            h, r = divmod(j, 8)
            inverse = 1.0 / along_rows(cols[h][j], r)

            def sweep(pair):
                turned = along_rows(pair[h], r) * inverse
                new = [pair[t] - cols[t][j] * turned for t in range(2)]
                new[h] = jnp.where(on[r], turned, new[h])
                return new

            for m in range(j + 1, 16):
                cols[0][m], cols[1][m] = sweep((cols[0][m], cols[1][m]))
            work = sweep(work)
        spread = [along_rows(work[j // 8], j % 8) for j in range(16)]
        near = [2 * p + 2, 2 * p + 3] if p < 7 else []
        rest = [q for q in range(16) if q not in near and q // 2 != p]
        new = {}
        for q in near:
            new[q] = jnp.where(inside, 0.0, tiles[q]) - tree_sum(
                [along_lanes(tiles[q], base + j) * spread[j] for j in range(16)]
            )
        left = jnp.concatenate([tiles[q] for q in rest], axis=0)
        right = jnp.concatenate([work[q - 2 * p] if q // 2 == p else zero for q in range(16)], axis=0)
        product = dot(left, right, ((1,), (0,)))
        for i, q in enumerate(rest):
            new[q] = jnp.where(inside, 0.0, tiles[q]) - product[8 * i : 8 * i + 8]
        for q in new:
            tiles[q] = new[q]
        tiles[2 * p : 2 * p + 2] = work
    return tiles


def shift_matrix():
    return jnp.where(
        lax.broadcasted_iota(jnp.int32, (128, 128), 0) == lax.broadcasted_iota(jnp.int32, (128, 128), 1),
        REG_SHIFT, 0.0,
    ).astype(F32)


def solve(first, above, second, fin, own, coeff_ref, rows, samp):
    B = 128
    blocks = {(a, b): gram_block(fin, a, b) for a in range(4) for b in range(a, 4)}

    energies = fin[0, HALF:PART, :] + fin[1, HALF:PART, :]
    mean = jnp.sum(energies, axis=(0, 1), keepdims=True) / TOTAL
    rhs = [jnp.broadcast_to(energies[a : a + 1, :] - mean, (8, B)) for a in range(4)]

    upper = {}
    sol = {}
    for s in range(4):
        p = (first, second)[s] if s < 2 else join(invert(split(blocks[s, s])))
        for j in range(s + 1, 4):
            upper[s, j] = above if (s, j) == (0, 1) else dot(p, blocks[s, j], ((1,), (0,)))
            for i in range(s + 1, j + 1):
                if (s, i, j) == (0, 1, 1):
                    continue
                blocks[i, j] = blocks[i, j] - dot(blocks[s, i], upper[s, j], ((0,), (0,)))
        sol[s] = dot(rhs[s], p, ((1,), (0,)))
        for j in range(s + 1, 4):
            rhs[j] = rhs[j] - dot(sol[s], blocks[s, j], ((1,), (0,)))
        for i in range(s):
            sol[i] = sol[i] - dot(sol[s], upper[i, s], ((1,), (1,)))
            for j in range(s + 1, 4):
                upper[i, j] = upper[i, j] - dot(upper[i, s], upper[s, j], ((1,), (0,)))

    scale = -math.sqrt(PARAMS / TOTAL)
    mine = sol[0]
    for a in range(1, 4):
        mine = jnp.where(samp // 8 == a, sol[a], mine)
    coeff_ref[...] = pltpu.roll(mine, (128 - OWN * (samp % 8)) % 128, 1)[0:1, 0:OWN]
    coeffs = jnp.concatenate([sol[a] for a in range(4)], axis=1)
    high = coeffs.astype(BF16).astype(F32)
    middle = (coeffs - high).astype(BF16).astype(F32)
    low = coeffs - high - middle
    terms = jnp.concatenate([high, middle, low, jnp.zeros((8, TOTAL), F32)], axis=0).astype(BF16)
    for slot in range(2):
        total = lax.dot_general(terms, own[slot], (((1,), (0,)), ((), ())), preferred_element_type=F32)
        rows[slot] = scale * (total[0:8] + (total[8:16] + total[16:24]))


def local(activations, cotangents, energies):
    act = activations.reshape(OWN, LANES, SITES)
    rows, coeffs = whole(act, cotangents, energies.reshape(1, OWN))
    update = rows.transpose(0, 2, 1).reshape(OUT_OWN, -1)
    return update, coeffs.reshape(OWN)


def solution(mesh):
    return jax.shard_map(
        local,
        mesh=mesh,
        in_specs=(P("samp", None, None, None), P("samp", None, "par", None), P("samp")),
        out_specs=(P("par", None), P("samp")),
        check_vma=False,
    )
```
